32 devices in a mesh: clique: 4 (over y, x), group: 8 (over z, core).
Axes of the slice: x: 2, y: 2, z: 4, core: 2. Of those that a mesh axis runs over, the one named last changes fastest.
Arguments:
- hot_shard: bfloat16 [65536, 128], P('clique'), may hold values from -6 to 6
- cold_shard: bfloat16 [131072, 128], P('group'), may hold values from -6 to 6
- hot_ids: int32 [32, 4, 512], P(('clique', 'group')), may hold values from 0 to 16383
- cold_ids: int32 [32, 8, 256], P(('clique', 'group')), may hold values from 0 to 16383
- cold_counts: int32 [32, 8], P(('clique', 'group')), may hold values from 128 to 256, as said below
- mid_self: int32 [32, 7680], P(('clique', 'group')), may hold values from 0 to 4095, as said below
- nbr1: int32 [32, 10, 7680], P(('clique', 'group')), may hold values from 0 to 4095, as said below
- nbr2: int32 [32, 15, 512], P(('clique', 'group')), may hold values from 0 to 7679
- labels: int32 [32, 512], P(('clique', 'group')), may hold values from 0 to 171
- w1_self: bfloat16 [128, 256], replicated, may hold values from -0.5 to 0.5
- w1_neigh: bfloat16 [128, 256], replicated, may hold values from -0.5 to 0.5
- w2_self: bfloat16 [256, 172], replicated, may hold values from -1.5 to 1.5
- w2_neigh: bfloat16 [256, 172], replicated, may hold values from -1.5 to 1.5
Outputs:
- seed_loss: float32 [32, 512], P(('clique', 'group'))
- grad_w1_self: float32 [128, 256], replicated
- grad_w1_neigh: float32 [128, 256], replicated
- grad_w2_self: float32 [256, 172], replicated
- grad_w2_neigh: float32 [256, 172], replicated
The draws below stay inside these ranges and needn't reach their ends.
Inputs may be any that keep to these rules, and one draw needn't show every extreme that they name: `cold_counts`: the last store device has 256 live slots from every trainer; the other counts vary from store device to store device. `mid_self`: each entry is a position in the trainer's inputs that holds a hot row or a live cold slot. `nbr1`: each entry is a position in the trainer's inputs that holds a hot row or a live cold slot.
All inputs are finite; a program needn't handle non-finite values.
Results may differ from the reference program's by a relative error of at most 0.0021.
Values may be sent and summed in bfloat16 or wider, within the bound.
A program may use at most 128 MiB of HBM per device.

```python
from functools import partial
import jax
import jax.numpy as jnp
from jax import lax

F = 128
HID = 256
CLASSES = 172
FAN0 = 10
FAN1 = 15
SEEDS = 512
HOT_ROWS = 2048
COLD_ROWS = 2048
HOT_SHARD = 16384
COLD_SHARD = 16384
MID = 7680
HOT_SLOT = 512
COLD_SLOT = 256
HOT_TABLE = 65536
COLD_TABLE = 131072
N_CLIQUE = 4
N_GROUP = 8
DEVICES = 32


def shared_counts(key):
    key = jax.random.fold_in(key, 101)
    second, third = jax.random.split(key, 2)
    weights = jax.random.randint(second, (N_GROUP,), 1, 4)
    raw_counts = jax.random.randint(third, (DEVICES, N_GROUP), COLD_SLOT // 2, COLD_SLOT + 1)
    counts = jnp.minimum(raw_counts * weights[None, :], COLD_SLOT)
    owners = jnp.arange(N_GROUP, dtype=jnp.int32)[None, :]
    return jnp.where(owners == N_GROUP - 1, COLD_SLOT, counts).astype(jnp.int32)


def live_positions(key, counts, tail):
    totals = HOT_ROWS + jnp.sum(counts, axis=1)

    def one_trainer(subkey, row_counts, row_total):
        picks = jax.random.randint(subkey, tail, 0, row_total)
        bounds = jnp.cumsum(row_counts)
        offset = picks - HOT_ROWS
        owner = jnp.clip(jnp.searchsorted(bounds, offset, side='right'), 0, N_GROUP - 1)
        start = bounds[owner] - row_counts[owner]
        cold_pos = HOT_ROWS + owner * COLD_SLOT + offset - start
        chosen = jnp.where(picks < HOT_ROWS, picks, cold_pos).astype(jnp.int32)
        flat = chosen.reshape(-1)
        flat = flat.at[0].set(0)
        flat = flat.at[-1].set(HOT_ROWS + COLD_ROWS - 1)
        return flat.reshape(tail)
    subkeys = jax.random.split(key, DEVICES)
    return jax.vmap(one_trainer)(subkeys, counts, totals)


def draw_cold_counts(key, part):
    counts = shared_counts(key)
    return counts


def draw_mid_self(key, part):
    counts = shared_counts(key)
    key = jax.random.fold_in(key, 2)
    return live_positions(key, counts, (MID,))


def draw_nbr1(key, part):
    counts = shared_counts(key)
    key = jax.random.fold_in(key, 3)
    return live_positions(key, counts, (FAN0, MID))


def plant(values, key, low, top_value):
    longest = values.shape.index(max(values.shape))
    spots = []
    for shift in (0, 1):
        where = [jax.random.randint(jax.random.fold_in(key, axis), (), 0, length) for axis, length in enumerate(values.shape)]
        where[longest] = (where[longest] + shift) % values.shape[longest]
        spots.append(tuple(where))
    return values.at[spots[0]].set(low).at[spots[1]].set(top_value)


def level_of(own_key, extent, cuts, smallest, top_value):
    gain, own = 1.0, jax.random.fold_in(own_key, 6)
    for axis_at, shards_of in cuts:
        steps = jnp.exp(jax.random.uniform(jax.random.fold_in(own, axis_at), (shards_of,), jnp.float32, smallest / len(cuts), top_value / len(cuts)))
        gain = gain * jnp.repeat(steps, extent[axis_at] // shards_of).reshape([-1 if axis == axis_at else 1 for axis in range(len(extent))])
    return gain


def noise(own_key, dims, width, bound, cuts=(), kind=jnp.bfloat16):
    result = jax.random.normal(own_key, dims, jnp.float32) * width
    if len(cuts) > 0:
        result = level_of(own_key, dims, cuts, -0.22, 0.18) * result
    return jnp.clip(result, min=-bound, max=bound).astype(kind)


def setup_inputs(seed: int = 0) -> dict:
    streams_of = jax.random.split(jax.random.key(seed), 14)
    return {
        "hot_shard": noise(streams_of[0], (HOT_TABLE, F), 1.0, 6.0, ((0, 4),)),
        "cold_shard": noise(streams_of[1], (COLD_TABLE, F), 1.0, 6.0, ((0, 8),)),
        "hot_ids": plant(jax.random.randint(streams_of[2], (DEVICES, N_CLIQUE, HOT_SLOT), 0, HOT_SHARD), jax.random.fold_in(streams_of[2], 1), 0, HOT_SHARD - 1).astype(jnp.int32),
        "cold_ids": plant(jax.random.randint(streams_of[3], (DEVICES, N_GROUP, COLD_SLOT), 0, COLD_SHARD), jax.random.fold_in(streams_of[3], 1), 0, COLD_SHARD - 1).astype(jnp.int32),
        "cold_counts": draw_cold_counts(jax.random.fold_in(streams_of[13], 71), 0),
        "mid_self": draw_mid_self(jax.random.fold_in(streams_of[13], 71), 0),
        "nbr1": draw_nbr1(jax.random.fold_in(streams_of[13], 71), 0),
        "nbr2": plant(jax.random.randint(streams_of[7], (DEVICES, FAN1, SEEDS), 0, MID), jax.random.fold_in(streams_of[7], 1), 0, MID - 1).astype(jnp.int32),
        "labels": plant(jax.random.randint(streams_of[8], (DEVICES, SEEDS), 0, CLASSES), jax.random.fold_in(streams_of[8], 1), 0, CLASSES - 1).astype(jnp.int32),
        "w1_self": noise(streams_of[9], (F, HID), F ** -0.5, 0.5),
        "w1_neigh": noise(streams_of[10], (F, HID), F ** -0.5, 0.5),
        "w2_self": noise(streams_of[11], (HID, CLASSES), (HID // 16) ** -0.5, 1.5),
        "w2_neigh": noise(streams_of[12], (HID, CLASSES), (HID // 16) ** -0.5, 1.5),
    }


def sage_step(self_first, neigh_first, seed_neigh, seed_labels, w1_self, w1_neigh, w2_self, w2_neigh):
    seeds = seed_labels.shape[0]
    fan_second = seed_neigh.shape[0]
    middle = self_first.shape[0]
    hidden = w1_self.shape[1]
    classes = w2_self.shape[1]
    pre_first = jnp.dot(self_first, w1_self, preferred_element_type=jnp.float32) + jnp.dot(neigh_first, w1_neigh, preferred_element_type=jnp.float32)
    hidden_first = jax.nn.gelu(pre_first, approximate=True).astype(jnp.bfloat16)
    gathered = jnp.take(hidden_first, seed_neigh, axis=0)
    neigh_second = (lax.optimization_barrier(jnp.sum(gathered, axis=0, dtype=jnp.float32)) / fan_second).astype(jnp.bfloat16)
    seed_hidden = hidden_first[:seeds]
    logits = jnp.dot(seed_hidden, w2_self, preferred_element_type=jnp.float32) + jnp.dot(neigh_second, w2_neigh, preferred_element_type=jnp.float32)
    log_total = jnp.log(lax.optimization_barrier(jnp.sum(jnp.exp(logits), axis=1)))
    picked = jnp.take_along_axis(logits, seed_labels[:, None], axis=1)[:, 0]
    seed_loss = log_total - picked
    onehot = (seed_labels[:, None] == jnp.arange(classes, dtype=jnp.int32)[None, :]).astype(jnp.float32)
    probs = jnp.exp(logits - log_total[:, None])
    grad_logits = ((probs - onehot) / seeds).astype(jnp.bfloat16)
    term_w2_self = jnp.dot(seed_hidden.T, grad_logits, preferred_element_type=jnp.float32)
    term_w2_neigh = jnp.dot(neigh_second.T, grad_logits, preferred_element_type=jnp.float32)
    back_second = jnp.dot(grad_logits, w2_neigh.T, preferred_element_type=jnp.float32) / fan_second
    spread = jnp.broadcast_to(back_second[None], (fan_second, seeds, hidden)).reshape(-1, hidden)
    grad_hidden = jnp.zeros((middle, hidden), jnp.float32).at[seed_neigh.reshape(-1)].add(spread)
    grad_hidden = grad_hidden.at[:seeds].add(jnp.dot(grad_logits, w2_self.T, preferred_element_type=jnp.float32))
    unused, pullback = jax.vjp(partial(jax.nn.gelu, approximate=True), pre_first)
    grad_pre = pullback(grad_hidden)[0].astype(jnp.bfloat16)
    term_w1_self = jnp.dot(self_first.T, grad_pre, preferred_element_type=jnp.float32)
    term_w1_neigh = jnp.dot(neigh_first.T, grad_pre, preferred_element_type=jnp.float32)
    return (seed_loss, term_w1_self, term_w1_neigh, term_w2_self, term_w2_neigh)

def reference(hot_shard, cold_shard, hot_ids, cold_ids, cold_counts, mid_self, nbr1, nbr2, labels, w1_self, w1_neigh, w2_self, w2_neigh):

    def one_trainer(packed):
        hot_index, cold_index, counts, self_index, neigh_index, seed_neigh, seed_labels = packed
        hot_pos = (jnp.arange(N_CLIQUE, dtype=jnp.int32)[:, None] * HOT_SHARD + hot_index).reshape(-1)
        hot_rows = jnp.take(hot_shard, hot_pos, axis=0)
        cold_pos = (jnp.arange(N_GROUP, dtype=jnp.int32)[:, None] * COLD_SHARD + cold_index).reshape(-1)
        cold_rows = jnp.take(cold_shard, cold_pos, axis=0)
        live_mask = (jnp.arange(COLD_SLOT, dtype=jnp.int32)[None, :] < counts[:, None]).reshape(-1)
        cold_rows = jnp.where(live_mask[:, None], cold_rows, jnp.zeros_like(cold_rows))
        inputs = jnp.concatenate([hot_rows, cold_rows], axis=0)
        self_first = jnp.take(inputs, self_index, axis=0)
        neigh_first = (lax.optimization_barrier(jnp.sum(jnp.take(inputs, neigh_index, axis=0), axis=0, dtype=jnp.float32)) / FAN0).astype(jnp.bfloat16)
        return sage_step(self_first, neigh_first, seed_neigh, seed_labels, w1_self, w1_neigh, w2_self, w2_neigh)
    losses, terms_a, terms_b, terms_c, terms_d = lax.map(one_trainer, (hot_ids, cold_ids, cold_counts, mid_self, nbr1, nbr2, labels))
    return (losses, lax.optimization_barrier(jnp.sum(terms_a, axis=0)), lax.optimization_barrier(jnp.sum(terms_b, axis=0)), lax.optimization_barrier(jnp.sum(terms_c, axis=0)), lax.optimization_barrier(jnp.sum(terms_d, axis=0)))
```

```python
from functools import partial

import jax
import jax.numpy as jnp
from jax import lax
from jax.experimental import pallas as pl
from jax.experimental.pallas import tpu as pltpu
from jax.sharding import PartitionSpec as P

GELU_SCALE = 0.7978845608028654
GELU_CUBE = 0.044715
GRAD_ROWS = 1280
MESH = pl.DeviceIdType.MESH


def dot_first(left, right):
    return lax.dot_general(
        left, right, (((0,), (0,)), ((), ())), preferred_element_type=jnp.float32
    )


def dot_last(left, right):
    return lax.dot_general(
        left, right, (((1,), (1,)), ((), ())), preferred_element_type=jnp.float32
    )


def sage_kernel(
    counts_ref,
    self_ref,
    nbr1_ref,
    nbr2_ref,
    hot_ref,
    cold_ref,
    nbr2_vec_ref,
    labels_ref,
    w1_self_ref,
    w1_neigh_ref,
    w2_self_ref,
    w2_neigh_ref,
    loss_ref,
    grads_ref,
    table,
    spread_ids,
    self_rows,
    sum_rows,
    self_all,
    neigh_all,
    slope_all,
    hidden_all,
    counts_t,
    second_sum,
    w2_pad,
):
    step = pl.program_id(0)
    steps = pl.num_programs(0)
    fan_first, block = nbr1_ref.shape[1], nbr1_ref.shape[2]
    fan_second, seeds = nbr2_ref.shape[1], nbr2_ref.shape[2]
    owners, slots, width = cold_ref.shape
    hot_rows = hot_ref.shape[0]
    hidden = w1_self_ref.shape[1]
    classes = w2_self_ref.shape[1]
    padded = w2_pad.shape[2]

    @pl.when(step == 0)
    def _():
        table[0:hot_rows, :] = hot_ref[...].astype(jnp.float32)

        @pl.loop(0, owners)
        def _(owner):
            live = lax.broadcasted_iota(jnp.int32, (slots, width), 0) < counts_ref[0, owner]
            rows = cold_ref[owner].astype(jnp.float32)
            start = pl.multiple_of(hot_rows + owner * slots, 8)
            table[pl.ds(start, slots), :] = jnp.where(live, rows, 0.0)

        for k in range(fan_second):
            spread_ids[k] = jnp.broadcast_to(nbr2_vec_ref[0, k : k + 1, :], (8, seeds))
        w2_pad[...] = jnp.zeros_like(w2_pad)
        w2_pad[0, :, 0:classes] = w2_self_ref[...]
        w2_pad[1, :, 0:classes] = w2_neigh_ref[...]

    node_base = step * block

    @pl.loop(0, block // 16)
    def _(group):
        row = pl.multiple_of(group * 16, 16)
        for r in range(16):
            total = table[pl.ds(nbr1_ref[0, 0, row + r], 1), :]
            for k in range(1, fan_first):
                total = total + table[pl.ds(nbr1_ref[0, k, row + r], 1), :]
            sum_rows[pl.ds(row + r, 1), :] = total
            self_rows[pl.ds(row + r, 1), :] = table[pl.ds(self_ref[0, row + r], 1), :]
        halves = []
        for half in range(2):
            node = lax.broadcasted_iota(jnp.int32, (8, seeds), 0) + (node_base + row + half * 8)
            seen = jnp.zeros((8, seeds), jnp.float32)
            for k in range(fan_second):
                seen = seen + jnp.where(spread_ids[k] == node, 1.0, 0.0)
            halves.append(seen)
        counts_t[pl.ds(pl.multiple_of(node_base + row, 16), 16), :] = jnp.concatenate(
            halves, axis=0
        ).astype(jnp.bfloat16)

    here = pl.ds(pl.multiple_of(node_base, block), block)
    self_first = self_rows[...].astype(jnp.bfloat16)
    neigh_first = (sum_rows[...] / fan_first).astype(jnp.bfloat16)
    self_all[here, :] = self_first
    neigh_all[here, :] = neigh_first
    pre = jnp.dot(self_first, w1_self_ref[...], preferred_element_type=jnp.float32) + jnp.dot(
        neigh_first, w1_neigh_ref[...], preferred_element_type=jnp.float32
    )
    square = pre * pre
    bend = jnp.tanh(GELU_SCALE * (pre + GELU_CUBE * (square * pre)))
    half_up = 0.5 * (1.0 + bend)
    hidden_all[here, :] = (pre * half_up).astype(jnp.bfloat16).astype(jnp.float32)
    slope_all[here, :] = half_up + (0.5 * GELU_SCALE) * pre * (1.0 - bend * bend) * (
        1.0 + (3.0 * GELU_CUBE) * square
    )

    @pl.when(step == steps - 1)
    def _():
        @pl.loop(0, seeds // 8)
        def _(group):
            row = pl.multiple_of(group * 8, 8)
            for r in range(8):
                total = hidden_all[pl.ds(nbr2_ref[0, 0, row + r], 1), :]
                for k in range(1, fan_second):
                    total = total + hidden_all[pl.ds(nbr2_ref[0, k, row + r], 1), :]
                second_sum[pl.ds(row + r, 1), :] = total

        neigh_second = (second_sum[...] / fan_second).astype(jnp.bfloat16)
        seed_hidden = hidden_all[0:seeds, :].astype(jnp.bfloat16)
        w2_self = w2_pad[0]
        w2_neigh = w2_pad[1]
        logits = jnp.dot(seed_hidden, w2_self, preferred_element_type=jnp.float32) + jnp.dot(
            neigh_second, w2_neigh, preferred_element_type=jnp.float32
        )
        column = lax.broadcasted_iota(jnp.int32, (seeds, padded), 1)
        real = column < classes
        log_total = jnp.log(
            jnp.sum(jnp.where(real, jnp.exp(logits), 0.0), axis=1, keepdims=True)
        )
        label = jnp.transpose(jnp.broadcast_to(labels_ref[...], (128, seeds)))
        label = jnp.concatenate([label] * (padded // 128), axis=1)
        onehot = jnp.where(column == label, 1.0, 0.0)
        picked = jnp.sum(onehot * logits, axis=1, keepdims=True)
        loss = jnp.broadcast_to(log_total - picked, (seeds, 128))
        loss_ref[...] = jnp.transpose(loss)[0:1, :]
        probs = jnp.where(real, jnp.exp(logits - log_total), 0.0)
        grad_logits = ((probs - onehot) / seeds).astype(jnp.bfloat16)
        term_self = dot_first(seed_hidden, grad_logits)
        term_neigh = dot_first(neigh_second, grad_logits)
        at = 4 * width
        grads_ref[at : at + hidden, :] = term_self[:, 0:128]
        grads_ref[at + hidden : at + 2 * hidden, :] = term_neigh[:, 0:128]
        grads_ref[at + 2 * hidden : at + 3 * hidden, :] = term_self[:, 128:256] + pltpu.roll(
            term_neigh[:, 128:256], 64, 1
        )
        back_second = dot_last(grad_logits, w2_neigh) / fan_second
        back_high = back_second.astype(jnp.bfloat16)
        back_low = (back_second - back_high.astype(jnp.float32)).astype(jnp.bfloat16)
        second_sum[...] = dot_last(grad_logits, w2_self)

        grads_ref[0:at, :] = jnp.zeros((at, 128), jnp.float32)

        @pl.loop(0, steps)
        def _(part):
            rows = pl.ds(pl.multiple_of(part * block, block), block)
            seen = counts_t[rows, :]
            grad = jnp.dot(seen, back_high, preferred_element_type=jnp.float32) + jnp.dot(
                seen, back_low, preferred_element_type=jnp.float32
            )
            own = jnp.where(part == 0, 1.0, 0.0)
            grad = grad + own * second_sum[...]
            grad_pre = (grad * slope_all[rows, :]).astype(jnp.bfloat16)
            first = dot_first(self_all[rows, :], grad_pre)
            other = dot_first(neigh_all[rows, :], grad_pre)
            grads_ref[0:width, :] += first[:, 0:128]
            grads_ref[width : 2 * width, :] += first[:, 128:256]
            grads_ref[2 * width : 3 * width, :] += other[:, 0:128]
            grads_ref[3 * width : 4 * width, :] += other[:, 128:256]


def sage_step(hot_rows, cold_rows, counts, mid_self, nbr1, nbr2, labels, weights):
    w1_self, w1_neigh, w2_self, w2_neigh = weights
    seeds = labels.shape[1]
    middle = mid_self.shape[1]
    fan_first, fan_second = nbr1.shape[1], nbr2.shape[1]
    width, hidden = w1_self.shape
    block = seeds
    steps = middle // block
    table_rows = hot_rows.shape[0] + cold_rows.shape[0] * cold_rows.shape[1]
    vmem = pl.BlockSpec(memory_space=pltpu.VMEM)
    smem = pl.BlockSpec(memory_space=pltpu.SMEM)
    return pl.pallas_call(
        sage_kernel,
        grid=(steps,),
        out_shape=(
            jax.ShapeDtypeStruct((1, seeds), jnp.float32),
            jax.ShapeDtypeStruct((GRAD_ROWS, 128), jnp.float32),
        ),
        in_specs=[
            smem,
            pl.BlockSpec((1, block), lambda i: (0, i), memory_space=pltpu.SMEM),
            pl.BlockSpec((1, fan_first, block), lambda i: (0, 0, i), memory_space=pltpu.SMEM),
            smem,
        ]
        + [vmem] * 8,
        out_specs=(vmem, vmem),
        scratch_shapes=[
            pltpu.VMEM((table_rows, width), jnp.float32),
            pltpu.VMEM((fan_second, 8, seeds), jnp.int32),
            pltpu.VMEM((block, width), jnp.float32),
            pltpu.VMEM((block, width), jnp.float32),
            pltpu.VMEM((middle, width), jnp.bfloat16),
            pltpu.VMEM((middle, width), jnp.bfloat16),
            pltpu.VMEM((middle, hidden), jnp.float32),
            pltpu.VMEM((middle, hidden), jnp.float32),
            pltpu.VMEM((middle, seeds), jnp.bfloat16),
            pltpu.VMEM((seeds, hidden), jnp.float32),
            pltpu.VMEM((2, hidden, 256), jnp.bfloat16),
        ],
        compiler_params=pltpu.CompilerParams(vmem_limit_bytes=52 * 1024 * 1024),
        name="sage_step",
    )(
        counts, mid_self, nbr1, nbr2,
        hot_rows, cold_rows, nbr2, labels, w1_self, w1_neigh, w2_self, w2_neigh,
    )


def reduce_kernel(
    cliques,
    groups,
    term_ref,
    w1_self_ref,
    w1_neigh_ref,
    w2_self_ref,
    w2_neigh_ref,
    whole,
    pair_in,
    clique_in,
    chip_in,
    half_sum,
    back,
    pair_sems,
    clique_sems,
    chip_sems,
):
    chips = groups // 2
    c = lax.axis_index("clique")
    g = lax.axis_index("group")
    core = lax.rem(g, 2)
    chip = g // 2
    rows = whole.shape[0]
    per_pair = rows // 2
    per_clique = per_pair // cliques
    per_chip = per_clique // chips

    def pair():
        return (c, chip * 2 + 1 - core)

    def clique(d):
        return (lax.rem(c + d, cliques), g)

    def other_chip(d):
        return (c, lax.rem(chip + d, chips) * 2 + core)

    def rows_at(start, size):
        return pl.ds(pl.multiple_of(start, 8), size)

    def send(source, target, sems, number, device):
        copy = pltpu.make_async_remote_copy(
            src_ref=source,
            dst_ref=target,
            send_sem=sems.at[0, number],
            recv_sem=sems.at[1, number],
            device_id=device,
            device_id_type=MESH,
        )
        copy.start()
        return copy

    barrier = pltpu.get_barrier_semaphore()
    partners = [pair()]
    partners += [clique(d) for d in range(1, cliques)]
    partners += [other_chip(d) for d in range(1, chips)]
    for device in partners:
        pl.semaphore_signal(barrier, inc=1, device_id=device, device_id_type=MESH)
    terms = term_ref.shape[0]
    whole[0:terms, :] = term_ref[...]
    if rows > terms:
        whole[terms:rows, :] = jnp.zeros((rows - terms, 128), jnp.float32)
    pl.semaphore_wait(barrier, len(partners))

    pair_start = core * per_pair
    mine = pair_start + c * per_clique
    own = mine + chip * per_chip

    copy = send(
        whole.at[rows_at((1 - core) * per_pair, per_pair)], pair_in, pair_sems, 0, pair()
    )
    copy.wait()
    half = rows_at(pair_start, per_pair)
    half_sum[half, :] = whole[half, :] + pair_in[...]

    copies = []
    for d in range(1, cliques):
        peer = lax.rem(c + d, cliques)
        part = rows_at(pair_start + peer * per_clique, per_clique)
        copies.append(send(half_sum.at[part], clique_in.at[d - 1], clique_sems, d - 1, clique(d)))
    for copy in copies:
        copy.wait()
    part = rows_at(mine, per_clique)
    total = half_sum[part, :]
    for d in range(1, cliques):
        total = total + clique_in[d - 1]
    whole[part, :] = total

    copies = []
    for d in range(1, chips):
        peer = lax.rem(chip + d, chips)
        part = rows_at(mine + peer * per_chip, per_chip)
        copies.append(send(whole.at[part], chip_in.at[d - 1], chip_sems, d - 1, other_chip(d)))
    for copy in copies:
        copy.wait()
    part = rows_at(own, per_chip)
    total = whole[part, :]
    for d in range(1, chips):
        total = total + chip_in[d - 1]
    back[part, :] = total

    copies = []
    for d in range(1, chips):
        copies.append(
            send(back.at[part], back.at[part], chip_sems, chips - 2 + d, other_chip(d))
        )
    for copy in copies:
        copy.wait()
    part = rows_at(mine, per_clique)
    copies = []
    for d in range(1, cliques):
        copies.append(
            send(back.at[part], back.at[part], clique_sems, cliques - 2 + d, clique(d))
        )
    for copy in copies:
        copy.wait()
    part = rows_at(pair_start, per_pair)
    copy = send(back.at[part], back.at[part], pair_sems, 1, pair())
    copy.wait()

    width, hidden = w1_self_ref.shape
    tail = w2_self_ref.shape[1] - 128
    w1_self_ref[:, 0:128] = back[0:width, :]
    w1_self_ref[:, 128:256] = back[width : 2 * width, :]
    w1_neigh_ref[:, 0:128] = back[2 * width : 3 * width, :]
    w1_neigh_ref[:, 128:256] = back[3 * width : 4 * width, :]
    at = 4 * width
    w2_self_ref[:, 0:128] = back[at : at + hidden, :]
    w2_neigh_ref[:, 0:128] = back[at + hidden : at + 2 * hidden, :]
    tails = back[at + 2 * hidden : at + 3 * hidden, :]
    w2_self_ref[:, 128 : 128 + tail] = tails[:, 0:tail]
    w2_neigh_ref[:, 128 : 128 + tail] = pltpu.roll(tails, 64, 1)[:, 0:tail]


def reduce_terms(terms, shapes, cliques, groups):
    chips = groups // 2
    unit = 8 * 2 * cliques * chips
    rows = -(-terms.shape[0] // unit) * unit
    per_clique = rows // 2 // cliques
    vmem = pl.BlockSpec(memory_space=pltpu.VMEM)
    return pl.pallas_call(
        partial(reduce_kernel, cliques, groups),
        out_shape=tuple(jax.ShapeDtypeStruct(shape, jnp.float32) for shape in shapes),
        in_specs=[vmem],
        out_specs=(vmem,) * len(shapes),
        scratch_shapes=[
            pltpu.VMEM((rows, 128), jnp.float32),
            pltpu.VMEM((rows // 2, 128), jnp.float32),
            pltpu.VMEM((cliques - 1, per_clique, 128), jnp.float32),
            pltpu.VMEM((chips - 1, per_clique // chips, 128), jnp.float32),
            pltpu.VMEM((rows, 128), jnp.float32),
            pltpu.VMEM((rows, 128), jnp.float32),
            pltpu.SemaphoreType.DMA((2, 2)),
            pltpu.SemaphoreType.DMA((2, 2 * (cliques - 1))),
            pltpu.SemaphoreType.DMA((2, 2 * (chips - 1))),
        ],
        compiler_params=pltpu.CompilerParams(
            collective_id=0, has_side_effects=True, vmem_limit_bytes=32 * 1024 * 1024
        ),
        name="reduce_terms",
    )(terms)


def body(
    cliques,
    groups,
    hot_shard,
    cold_shard,
    hot_ids,
    cold_ids,
    cold_counts,
    mid_self,
    nbr1,
    nbr2,
    labels,
    w1_self,
    w1_neigh,
    w2_self,
    w2_neigh,
):
    width = hot_shard.shape[1]
    requests = lax.all_to_all(hot_ids[0], "clique", split_axis=0, concat_axis=0, tiled=True)
    served = jnp.take(hot_shard, requests, axis=0)
    hot_rows = lax.all_to_all(served, "clique", split_axis=0, concat_axis=0, tiled=True).reshape(
        -1, width
    )
    fetched = lax.all_to_all(
        jnp.take(
            cold_shard,
            lax.all_to_all(cold_ids[0], "group", split_axis=0, concat_axis=0, tiled=True),
            axis=0,
        ),
        "group",
        split_axis=0,
        concat_axis=0,
        tiled=True,
    )
    seed_loss, terms = sage_step(
        hot_rows, fetched, cold_counts, mid_self, nbr1, nbr2, labels,
        (w1_self, w1_neigh, w2_self, w2_neigh),
    )
    shapes = (w1_self.shape, w1_neigh.shape, w2_self.shape, w2_neigh.shape)
    totals = reduce_terms(terms, shapes, cliques, groups)
    return (seed_loss, totals[0], totals[1], totals[2], totals[3])


def solution(mesh):
    return jax.shard_map(
        partial(body, mesh.shape["clique"], mesh.shape["group"]),
        mesh=mesh,
        in_specs=(
            P("clique", None),
            P("group", None),
            P(("clique", "group"), None, None),
            P(("clique", "group"), None, None),
            P(("clique", "group"), None),
            P(("clique", "group"), None),
            P(("clique", "group"), None, None),
            P(("clique", "group"), None, None),
            P(("clique", "group"), None),
            P(),
            P(),
            P(),
            P(),
        ),
        out_specs=(P(("clique", "group"), None), P(), P(), P(), P()),
        check_vma=False,
    )
```

```python
from functools import partial

import jax
import jax.numpy as jnp
from jax import lax
from jax.experimental import pallas as pl
from jax.experimental.pallas import tpu as pltpu
from jax.sharding import PartitionSpec as P

GELU_SCALE = 0.7978845608028654
GELU_CUBE = 0.044715
GRAD_ROWS = 1280
MESH = pl.DeviceIdType.MESH


def dot_first(left, right):
    return lax.dot_general(
        left, right, (((0,), (0,)), ((), ())), preferred_element_type=jnp.float32
    )


def dot_last(left, right):
    return lax.dot_general(
        left, right, (((1,), (1,)), ((), ())), preferred_element_type=jnp.float32
    )


def sage_kernel(
    counts_ref,
    self_ref,
    nbr1_ref,
    hot_ref,
    cold_ref,
    nbr2_ref,
    labels_ref,
    w1_self_ref,
    w1_neigh_ref,
    w2_self_ref,
    w2_neigh_ref,
    loss_ref,
    grads_ref,
    table,
    spread_ids,
    self_rows,
    sum_rows,
    first_all,
    slope_all,
    counts_t,
    seed_hidden_ref,
    second_t,
    seed_grad,
    w1_both,
    w2_pad,
    grad_w1,
):
    step = pl.program_id(0)
    steps = pl.num_programs(0)
    groups, unit, width = sum_rows.shape
    block = groups * unit
    fan_first = nbr1_ref.shape[0] // block
    fan_second, seeds = nbr2_ref.shape[1], nbr2_ref.shape[2]
    owners, slots, _ = cold_ref.shape
    hot_rows = hot_ref.shape[0]
    hidden = w1_self_ref.shape[1]
    classes = w2_self_ref.shape[1]
    padded = w2_pad.shape[2]

    @pl.when(step == 0)
    def _():
        @pl.loop(0, hot_rows // 16)
        def _(part):
            rows = hot_ref[pl.ds(pl.multiple_of(part * 16, 16), 16), :].astype(jnp.float32)
            for r in range(16):
                table[part * 16 + r] = rows[r : r + 1, :]

        @pl.loop(0, owners)
        def _(owner):
            live = lax.broadcasted_iota(jnp.int32, (slots, width), 0) < counts_ref[0, owner]
            rows = jnp.where(live, cold_ref[owner].astype(jnp.float32), 0.0)
            for r in range(slots):
                table[hot_rows + owner * slots + r] = rows[r : r + 1, :]

        for k in range(fan_second):
            spread_ids[k] = jnp.broadcast_to(nbr2_ref[0, k : k + 1, :], (8, seeds))
        w1_both[0:width, :] = w1_self_ref[...]
        w1_both[width : 2 * width, :] = w1_neigh_ref[...]
        w2_pad[...] = jnp.zeros_like(w2_pad)
        w2_pad[0, :, 0:classes] = w2_self_ref[...]
        w2_pad[1, :, 0:classes] = w2_neigh_ref[...]
        second_t[...] = jnp.zeros_like(second_t)

    node_base = step * block

    @pl.loop(0, groups)
    def _(group):
        row = group * unit
        for r in range(unit):
            total = table[nbr1_ref[row + r]]
            for k in range(1, fan_first):
                total = total + table[nbr1_ref[row + (k * block + r)]]
            sum_rows[group, r : r + 1, :] = total
            self_rows[group, r : r + 1, :] = table[self_ref[node_base + row + r]]
        halves = []
        for half in range(unit // 8):
            node = lax.broadcasted_iota(jnp.int32, (8, seeds), 0) + (node_base + row + half * 8)
            seen = jnp.zeros((8, seeds), jnp.float32)
            for k in range(fan_second):
                seen = seen + jnp.where(spread_ids[k] == node, 1.0, 0.0)
            halves.append(seen)
        counts_t[step * groups + group] = jnp.concatenate(halves, axis=0).astype(jnp.bfloat16)

    here = pl.ds(pl.multiple_of(node_base, block), block)
    self_first = self_rows[...].reshape(block, width).astype(jnp.bfloat16)
    neigh_first = (sum_rows[...].reshape(block, width) / fan_first).astype(jnp.bfloat16)
    first = jnp.concatenate([self_first, neigh_first], axis=1)
    first_all[here, :] = first
    pre = jnp.dot(first, w1_both[...], preferred_element_type=jnp.float32)
    square = pre * pre
    bend = jnp.tanh(GELU_SCALE * (pre + GELU_CUBE * (square * pre)))
    half_up = 0.5 * (1.0 + bend)
    hidden_first = (pre * half_up).astype(jnp.bfloat16)
    slope_all[here, :] = half_up + (0.5 * GELU_SCALE) * pre * (1.0 - bend * bend) * (
        1.0 + (3.0 * GELU_CUBE) * square
    )
    seen = counts_t[pl.ds(step * groups, groups)].reshape(block, seeds)
    second_t[...] += dot_first(hidden_first, seen)

    @pl.when(step == 0)
    def _():
        seed_hidden_ref[...] = hidden_first

    @pl.when(step == steps - 1)
    def _():
        neigh_second = (jnp.transpose(second_t[...]) / fan_second).astype(jnp.bfloat16)
        seed_hidden = seed_hidden_ref[...]
        w2_self = w2_pad[0]
        w2_neigh = w2_pad[1]
        logits = jnp.dot(seed_hidden, w2_self, preferred_element_type=jnp.float32) + jnp.dot(
            neigh_second, w2_neigh, preferred_element_type=jnp.float32
        )
        column = lax.broadcasted_iota(jnp.int32, (seeds, padded), 1)
        real = column < classes
        log_total = jnp.log(
            jnp.sum(jnp.where(real, jnp.exp(logits), 0.0), axis=1, keepdims=True)
        )
        label = jnp.transpose(jnp.broadcast_to(labels_ref[...], (128, seeds)))
        label = jnp.concatenate([label] * (padded // 128), axis=1)
        onehot = jnp.where(column == label, 1.0, 0.0)
        picked = jnp.sum(onehot * logits, axis=1, keepdims=True)
        loss = jnp.broadcast_to(log_total - picked, (seeds, 128))
        loss_ref[...] = jnp.transpose(loss)[0:1, :]
        probs = jnp.where(real, jnp.exp(logits - log_total), 0.0)
        grad_logits = ((probs - onehot) / seeds).astype(jnp.bfloat16)
        term_self = dot_first(seed_hidden, grad_logits)
        term_neigh = dot_first(neigh_second, grad_logits)
        at = 4 * width
        grads_ref[at : at + hidden, :] = term_self[:, 0:128]
        grads_ref[at + hidden : at + 2 * hidden, :] = term_neigh[:, 0:128]
        grads_ref[at + 2 * hidden : at + 3 * hidden, :] = term_self[:, 128:256] + pltpu.roll(
            term_neigh[:, 128:256], 64, 1
        )
        back_second = dot_last(grad_logits, w2_neigh) / fan_second
        back_high = back_second.astype(jnp.bfloat16)
        back_low = (back_second - back_high.astype(jnp.float32)).astype(jnp.bfloat16)
        seed_grad[...] = dot_last(grad_logits, w2_self)
        grad_w1[...] = jnp.zeros_like(grad_w1)

        @pl.loop(0, steps)
        def _(part):
            rows = pl.ds(pl.multiple_of(part * block, block), block)
            seen = counts_t[pl.ds(part * groups, groups)].reshape(block, seeds)
            grad = jnp.dot(seen, back_high, preferred_element_type=jnp.float32) + jnp.dot(
                seen, back_low, preferred_element_type=jnp.float32
            )
            own = jnp.where(part == 0, 1.0, 0.0)
            grad = grad + own * seed_grad[...]
            grad_pre = (grad * slope_all[rows, :]).astype(jnp.bfloat16)
            grad_w1[...] += dot_first(first_all[rows, :], grad_pre)

        grads_ref[0:width, :] = grad_w1[0:width, 0:128]
        grads_ref[width : 2 * width, :] = grad_w1[0:width, 128:256]
        grads_ref[2 * width : 3 * width, :] = grad_w1[width : 2 * width, 0:128]
        grads_ref[3 * width : 4 * width, :] = grad_w1[width : 2 * width, 128:256]


def sage_step(hot_rows, cold_rows, counts, mid_self, nbr1, nbr2, labels, weights):
    w1_self, w1_neigh, w2_self, w2_neigh = weights
    seeds = labels.shape[1]
    middle = mid_self.shape[1]
    fan_first, fan_second = nbr1.shape[1], nbr2.shape[1]
    width, hidden = w1_self.shape
    block = seeds
    steps = middle // block
    unit = 16
    table_rows = hot_rows.shape[0] + cold_rows.shape[0] * cold_rows.shape[1]
    positions = nbr1.reshape(fan_first, steps, block).transpose(1, 0, 2).reshape(-1)
    vmem = pl.BlockSpec(memory_space=pltpu.VMEM)
    smem = pl.BlockSpec(memory_space=pltpu.SMEM)
    return pl.pallas_call(
        sage_kernel,
        grid=(steps,),
        out_shape=(
            jax.ShapeDtypeStruct((1, seeds), jnp.float32),
            jax.ShapeDtypeStruct((GRAD_ROWS, 128), jnp.float32),
        ),
        in_specs=[
            smem,
            smem,
            pl.BlockSpec((fan_first * block,), lambda i: (i,), memory_space=pltpu.SMEM),
        ]
        + [vmem] * 8,
        out_specs=(vmem, vmem),
        scratch_shapes=[
            pltpu.VMEM((table_rows, 1, width), jnp.float32),
            pltpu.VMEM((fan_second, 8, seeds), jnp.int32),
            pltpu.VMEM((block // unit, unit, width), jnp.float32),
            pltpu.VMEM((block // unit, unit, width), jnp.float32),
            pltpu.VMEM((middle, 2 * width), jnp.bfloat16),
            pltpu.VMEM((middle, hidden), jnp.float32),
            pltpu.VMEM((middle // unit, unit, seeds), jnp.bfloat16),
            pltpu.VMEM((seeds, hidden), jnp.bfloat16),
            pltpu.VMEM((hidden, seeds), jnp.float32),
            pltpu.VMEM((seeds, hidden), jnp.float32),
            pltpu.VMEM((2 * width, hidden), jnp.bfloat16),
            pltpu.VMEM((2, hidden, 256), jnp.bfloat16),
            pltpu.VMEM((2 * width, hidden), jnp.float32),
        ],
        compiler_params=pltpu.CompilerParams(vmem_limit_bytes=52 * 1024 * 1024),
        name="sage_step",
    )(
        counts, mid_self.reshape(-1), positions,
        hot_rows, cold_rows, nbr2, labels, w1_self, w1_neigh, w2_self, w2_neigh,
    )


def fetch_kernel(
    cliques,
    groups,
    hot_table,
    cold_table,
    hot_ids_ref,
    cold_ids_ref,
    hot_out,
    cold_out,
    hot_raw,
    cold_raw,
    hot_wide,
    cold_wide,
    hot_ask,
    cold_ask,
    hot_req,
    cold_req,
    hot_req_s,
    cold_req_s,
    hot_stage,
    cold_stage,
    hot_send,
    cold_send,
    local_sems,
    hot_id_sems,
    cold_id_sems,
    hot_row_sems,
    cold_row_sems,
):
    c = lax.axis_index("clique")
    g = lax.axis_index("group")

    def clique_at(d):
        return (lax.rem(c + d, cliques), g)

    def group_at(d):
        return (c, lax.rem(g + d, groups))

    load_cold = pltpu.make_async_copy(cold_table, cold_raw, local_sems.at[0])
    load_hot = pltpu.make_async_copy(hot_table, hot_raw, local_sems.at[1])
    load_cold.start()
    load_hot.start()

    barrier = pltpu.get_barrier_semaphore()

    @pl.loop(1, cliques)
    def _(d):
        pl.semaphore_signal(barrier, inc=1, device_id=clique_at(d), device_id_type=MESH)

    @pl.loop(1, groups)
    def _(d):
        pl.semaphore_signal(barrier, inc=1, device_id=group_at(d), device_id_type=MESH)

    for j in range(cliques):
        hot_ask[j] = hot_ids_ref[0, j : j + 1, :]
    for o in range(groups):
        cold_ask[o] = cold_ids_ref[0, o : o + 1, :]
    hot_req[c] = hot_ask[c]
    cold_req[g] = cold_ask[g]
    pl.semaphore_wait(barrier, cliques + groups - 2)

    def remote(source, target, sems, d, device):
        return pltpu.make_async_remote_copy(
            src_ref=source,
            dst_ref=target,
            send_sem=sems.at[0, d - 1],
            recv_sem=sems.at[1, d - 1],
            device_id=device,
            device_id_type=MESH,
        )

    def ask_cold(d):
        peer = lax.rem(g + d, groups)
        return remote(cold_ask.at[peer], cold_req.at[g], cold_id_sems, d, group_at(d))

    def ask_hot(d):
        peer = lax.rem(c + d, cliques)
        return remote(hot_ask.at[peer], hot_req.at[c], hot_id_sems, d, clique_at(d))

    def give_cold(d):
        peer = lax.rem(g + groups - d, groups)
        return remote(
            cold_send.at[peer], cold_out.at[g], cold_row_sems, d, group_at(groups - d)
        )

    def give_hot(d):
        peer = lax.rem(c + cliques - d, cliques)
        return remote(
            hot_send.at[peer], hot_out.at[c], hot_row_sems, d, clique_at(cliques - d)
        )

    @pl.loop(1, groups)
    def _(d):
        ask_cold(d).start()

    @pl.loop(1, cliques)
    def _(d):
        ask_hot(d).start()

    def widen(raw, wide):
        rows = 256

        @pl.loop(0, raw.shape[0] // rows)
        def _(part):
            here = pl.ds(pl.multiple_of(part * rows, rows), rows)
            wide[here, :] = raw[here, :].astype(jnp.float32)

    def gather(wide, wanted, who, stage):
        units, unit, width = stage.shape

        @pl.loop(0, units)
        def _(part):
            for r in range(unit):
                stage[part, r : r + 1, :] = wide[pl.ds(wanted[who, 0, part * unit + r], 1), :]

        return stage[...].reshape(units * unit, width).astype(jnp.bfloat16)

    load_cold.wait()
    widen(cold_raw, cold_wide)

    @pl.loop(1, groups)
    def _(d):
        ask_cold(d).wait()

    to_scalars = pltpu.make_async_copy(cold_req, cold_req_s, local_sems.at[2])
    to_scalars.start()
    to_scalars.wait()

    @pl.loop(1, groups)
    def _(d):
        peer = lax.rem(g + groups - d, groups)
        cold_send[peer] = gather(cold_wide, cold_req_s, peer, cold_stage)
        give_cold(d).start()

    load_hot.wait()
    widen(hot_raw, hot_wide)

    @pl.loop(1, cliques)
    def _(d):
        ask_hot(d).wait()

    to_scalars = pltpu.make_async_copy(hot_req, hot_req_s, local_sems.at[3])
    to_scalars.start()
    to_scalars.wait()

    @pl.loop(1, cliques)
    def _(d):
        peer = lax.rem(c + cliques - d, cliques)
        hot_send[peer] = gather(hot_wide, hot_req_s, peer, hot_stage)
        give_hot(d).start()

    hot_out[c] = gather(hot_wide, hot_req_s, c, hot_stage)
    cold_out[g] = gather(cold_wide, cold_req_s, g, cold_stage)

    @pl.loop(1, cliques)
    def _(d):
        give_hot(d).wait()

    @pl.loop(1, groups)
    def _(d):
        give_cold(d).wait()


def fetch_rows(hot_shard, cold_shard, hot_ids, cold_ids, cliques, groups):
    width = hot_shard.shape[1]
    hot_slots, cold_slots = hot_ids.shape[2], cold_ids.shape[2]
    vmem = pl.BlockSpec(memory_space=pltpu.VMEM)
    anywhere = pl.BlockSpec(memory_space=pl.ANY)
    bf16, f32, i32 = jnp.bfloat16, jnp.float32, jnp.int32
    return pl.pallas_call(
        partial(fetch_kernel, cliques, groups),
        out_shape=(
            jax.ShapeDtypeStruct((cliques, hot_slots, width), bf16),
            jax.ShapeDtypeStruct((groups, cold_slots, width), bf16),
        ),
        in_specs=[anywhere, anywhere, vmem, vmem],
        out_specs=(vmem, vmem),
        scratch_shapes=[
            pltpu.VMEM(hot_shard.shape, bf16),
            pltpu.VMEM(cold_shard.shape, bf16),
            pltpu.VMEM(hot_shard.shape, f32),
            pltpu.VMEM(cold_shard.shape, f32),
            pltpu.VMEM((cliques, 1, hot_slots), i32),
            pltpu.VMEM((groups, 1, cold_slots), i32),
            pltpu.VMEM((cliques, 1, hot_slots), i32),
            pltpu.VMEM((groups, 1, cold_slots), i32),
            pltpu.SMEM((cliques, 1, hot_slots), i32),
            pltpu.SMEM((groups, 1, cold_slots), i32),
            pltpu.VMEM((hot_slots // 16, 16, width), f32),
            pltpu.VMEM((cold_slots // 16, 16, width), f32),
            pltpu.VMEM((cliques, hot_slots, width), bf16),
            pltpu.VMEM((groups, cold_slots, width), bf16),
            pltpu.SemaphoreType.DMA((4,)),
            pltpu.SemaphoreType.DMA((2, cliques - 1)),
            pltpu.SemaphoreType.DMA((2, groups - 1)),
            pltpu.SemaphoreType.DMA((2, cliques - 1)),
            pltpu.SemaphoreType.DMA((2, groups - 1)),
        ],
        compiler_params=pltpu.CompilerParams(
            collective_id=1, has_side_effects=True, vmem_limit_bytes=48 * 1024 * 1024
        ),
        name="fetch_rows",
    )(hot_shard, cold_shard, hot_ids, cold_ids)


def reduce_kernel(
    cliques,
    groups,
    term_ref,
    w1_self_ref,
    w1_neigh_ref,
    w2_self_ref,
    w2_neigh_ref,
    whole,
    pair_in,
    clique_in,
    chip_in,
    half_sum,
    back,
    pair_sems,
    clique_sems,
    chip_sems,
):
    chips = groups // 2
    c = lax.axis_index("clique")
    g = lax.axis_index("group")
    core = lax.rem(g, 2)
    chip = g // 2
    rows = whole.shape[0]
    per_pair = rows // 2
    per_clique = per_pair // cliques
    per_chip = per_clique // chips

    def pair():
        return (c, chip * 2 + 1 - core)

    def clique(d):
        return (lax.rem(c + d, cliques), g)

    def other_chip(d):
        return (c, lax.rem(chip + d, chips) * 2 + core)

    def rows_at(start, size):
        return pl.ds(pl.multiple_of(start, 8), size)

    def send(source, target, sems, number, device):
        copy = pltpu.make_async_remote_copy(
            src_ref=source,
            dst_ref=target,
            send_sem=sems.at[0, number],
            recv_sem=sems.at[1, number],
            device_id=device,
            device_id_type=MESH,
        )
        copy.start()
        return copy

    barrier = pltpu.get_barrier_semaphore()
    partners = [pair()]
    partners += [clique(d) for d in range(1, cliques)]
    partners += [other_chip(d) for d in range(1, chips)]
    for device in partners:
        pl.semaphore_signal(barrier, inc=1, device_id=device, device_id_type=MESH)
    terms = term_ref.shape[0]
    whole[0:terms, :] = term_ref[...]
    if rows > terms:
        whole[terms:rows, :] = jnp.zeros((rows - terms, 128), jnp.float32)
    pl.semaphore_wait(barrier, len(partners))

    pair_start = core * per_pair
    mine = pair_start + c * per_clique
    own = mine + chip * per_chip

    copy = send(
        whole.at[rows_at((1 - core) * per_pair, per_pair)], pair_in, pair_sems, 0, pair()
    )
    copy.wait()
    half = rows_at(pair_start, per_pair)
    half_sum[half, :] = whole[half, :] + pair_in[...]

    copies = []
    for d in range(1, cliques):
        peer = lax.rem(c + d, cliques)
        part = rows_at(pair_start + peer * per_clique, per_clique)
        copies.append(send(half_sum.at[part], clique_in.at[d - 1], clique_sems, d - 1, clique(d)))
    for copy in copies:
        copy.wait()
    part = rows_at(mine, per_clique)
    total = half_sum[part, :]
    for d in range(1, cliques):
        total = total + clique_in[d - 1]
    whole[part, :] = total

    copies = []
    for d in range(1, chips):
        peer = lax.rem(chip + d, chips)
        part = rows_at(mine + peer * per_chip, per_chip)
        copies.append(send(whole.at[part], chip_in.at[d - 1], chip_sems, d - 1, other_chip(d)))
    for copy in copies:
        copy.wait()
    part = rows_at(own, per_chip)
    total = whole[part, :]
    for d in range(1, chips):
        total = total + chip_in[d - 1]
    back[part, :] = total

    copies = []
    for d in range(1, chips):
        copies.append(
            send(back.at[part], back.at[part], chip_sems, chips - 2 + d, other_chip(d))
        )
    for copy in copies:
        copy.wait()
    part = rows_at(mine, per_clique)
    copies = []
    for d in range(1, cliques):
        copies.append(
            send(back.at[part], back.at[part], clique_sems, cliques - 2 + d, clique(d))
        )
    for copy in copies:
        copy.wait()
    part = rows_at(pair_start, per_pair)
    copy = send(back.at[part], back.at[part], pair_sems, 1, pair())
    copy.wait()

    width, hidden = w1_self_ref.shape
    tail = w2_self_ref.shape[1] - 128
    w1_self_ref[:, 0:128] = back[0:width, :]
    w1_self_ref[:, 128:256] = back[width : 2 * width, :]
    w1_neigh_ref[:, 0:128] = back[2 * width : 3 * width, :]
    w1_neigh_ref[:, 128:256] = back[3 * width : 4 * width, :]
    at = 4 * width
    w2_self_ref[:, 0:128] = back[at : at + hidden, :]
    w2_neigh_ref[:, 0:128] = back[at + hidden : at + 2 * hidden, :]
    tails = back[at + 2 * hidden : at + 3 * hidden, :]
    w2_self_ref[:, 128 : 128 + tail] = tails[:, 0:tail]
    w2_neigh_ref[:, 128 : 128 + tail] = pltpu.roll(tails, 64, 1)[:, 0:tail]


def reduce_terms(terms, shapes, cliques, groups):
    chips = groups // 2
    unit = 8 * 2 * cliques * chips
    rows = -(-terms.shape[0] // unit) * unit
    per_clique = rows // 2 // cliques
    vmem = pl.BlockSpec(memory_space=pltpu.VMEM)
    return pl.pallas_call(
        partial(reduce_kernel, cliques, groups),
        out_shape=tuple(jax.ShapeDtypeStruct(shape, jnp.float32) for shape in shapes),
        in_specs=[vmem],
        out_specs=(vmem,) * len(shapes),
        scratch_shapes=[
            pltpu.VMEM((rows, 128), jnp.float32),
            pltpu.VMEM((rows // 2, 128), jnp.float32),
            pltpu.VMEM((cliques - 1, per_clique, 128), jnp.float32),
            pltpu.VMEM((chips - 1, per_clique // chips, 128), jnp.float32),
            pltpu.VMEM((rows, 128), jnp.float32),
            pltpu.VMEM((rows, 128), jnp.float32),
            pltpu.SemaphoreType.DMA((2, 2)),
            pltpu.SemaphoreType.DMA((2, 2 * (cliques - 1))),
            pltpu.SemaphoreType.DMA((2, 2 * (chips - 1))),
        ],
        compiler_params=pltpu.CompilerParams(
            collective_id=0, has_side_effects=True, vmem_limit_bytes=32 * 1024 * 1024
        ),
        name="reduce_terms",
    )(terms)


def body(
    cliques,
    groups,
    hot_shard,
    cold_shard,
    hot_ids,
    cold_ids,
    cold_counts,
    mid_self,
    nbr1,
    nbr2,
    labels,
    w1_self,
    w1_neigh,
    w2_self,
    w2_neigh,
):
    hot_rows, cold_rows = fetch_rows(hot_shard, cold_shard, hot_ids, cold_ids, cliques, groups)
    seed_loss, terms = sage_step(
        hot_rows.reshape(-1, hot_shard.shape[1]), cold_rows, cold_counts, mid_self, nbr1, nbr2, labels,
        (w1_self, w1_neigh, w2_self, w2_neigh),
    )
    shapes = (w1_self.shape, w1_neigh.shape, w2_self.shape, w2_neigh.shape)
    totals = reduce_terms(terms, shapes, cliques, groups)
    return (seed_loss, totals[0], totals[1], totals[2], totals[3])


def solution(mesh):
    return jax.shard_map(
        partial(body, mesh.shape["clique"], mesh.shape["group"]),
        mesh=mesh,
        in_specs=(
            P("clique", None),
            P("group", None),
            P(("clique", "group"), None, None),
            P(("clique", "group"), None, None),
            P(("clique", "group"), None),
            P(("clique", "group"), None),
            P(("clique", "group"), None, None),
            P(("clique", "group"), None, None),
            P(("clique", "group"), None),
            P(),
            P(),
            P(),
            P(),
        ),
        out_specs=(P(("clique", "group"), None), P(), P(), P(), P()),
        check_vma=False,
    )
```

```python
from functools import partial

import jax
import jax.numpy as jnp
from jax import lax
from jax.experimental import pallas as pl
from jax.experimental.pallas import tpu as pltpu
from jax.sharding import PartitionSpec as P

GELU_SCALE = 0.7978845608028654
GELU_CUBE = 0.044715
GRAD_ROWS = 1280
MESH = pl.DeviceIdType.MESH


def dot_first(left, right):
    return lax.dot_general(
        left, right, (((0,), (0,)), ((), ())), preferred_element_type=jnp.float32
    )


def dot_last(left, right):
    return lax.dot_general(
        left, right, (((1,), (1,)), ((), ())), preferred_element_type=jnp.float32
    )


def sage_kernel(
    counts_ref,
    self_ref,
    nbr1_ref,
    hot_ref,
    cold_ref,
    nbr2_ref,
    labels_ref,
    w1_self_ref,
    w1_neigh_ref,
    w2_self_ref,
    w2_neigh_ref,
    loss_ref,
    grads_ref,
    table,
    spread_ids,
    self_even,
    sum_even,
    self_odd,
    sum_odd,
    first_all,
    slope_all,
    hidden_all,
    counts_t,
    second_t,
    seed_grad,
    w1_both,
    w2_pad,
    grad_w1,
):
    step = pl.program_id(0)
    steps = pl.num_programs(0)
    units, unit, width = sum_even.shape
    part_rows = units * unit
    middle = first_all.shape[0]
    block = middle // steps
    pairs = block // (2 * part_rows)
    fan_first = nbr1_ref.shape[0] // block
    fan_second, seeds = nbr2_ref.shape[1], nbr2_ref.shape[2]
    owners, slots, _ = cold_ref.shape
    hot_rows = hot_ref.shape[0]
    hidden = w1_self_ref.shape[1]
    classes = w2_self_ref.shape[0]
    padded = w2_pad.shape[1]
    count_type = spread_ids.dtype

    @pl.when(step == 0)
    def _():
        @pl.loop(0, hot_rows // 16)
        def _(part):
            rows = hot_ref[pl.ds(pl.multiple_of(part * 16, 16), 16), :].astype(jnp.float32)
            for r in range(16):
                table[part * 16 + r] = rows[r : r + 1, :]

        @pl.loop(0, owners)
        def _(owner):
            live = lax.broadcasted_iota(jnp.int32, (slots, width), 0) < counts_ref[0, owner]
            rows = jnp.where(live, cold_ref[owner].astype(jnp.float32), 0.0)
            for r in range(slots):
                table[hot_rows + owner * slots + r] = rows[r : r + 1, :]

        for k in range(fan_second):
            spread_ids[k] = jnp.broadcast_to(nbr2_ref[0, k : k + 1, :], (unit, seeds)).astype(
                count_type
            )
        w1_both[0:width, :] = w1_self_ref[...]
        w1_both[width : 2 * width, :] = w1_neigh_ref[...]
        w2_pad[...] = jnp.zeros_like(w2_pad)
        w2_pad[0, 0:classes, :] = w2_self_ref[...]
        w2_pad[1, 0:classes, :] = w2_neigh_ref[...]
        self_odd[...] = jnp.zeros_like(self_odd)
        sum_odd[...] = jnp.zeros_like(sum_odd)

    def gather(local, start, self_rows, sum_rows):
        for u in range(units):
            for r in range(unit):
                at = u * unit + r
                total = table[nbr1_ref[local + at]]
                for k in range(1, fan_first):
                    total = total + table[nbr1_ref[local + (k * block + at)]]
                sum_rows[u, r : r + 1, :] = total
                self_rows[u, r : r + 1, :] = table[self_ref[start + at]]
            node = (
                lax.broadcasted_iota(jnp.int32, (unit, seeds), 0) + (start + u * unit)
            ).astype(count_type)
            seen = jnp.zeros((unit, seeds), jnp.bfloat16)
            one = jnp.ones((unit, seeds), jnp.bfloat16)
            none = jnp.zeros((unit, seeds), jnp.bfloat16)
            for k in range(fan_second):
                seen = seen + jnp.where(spread_ids[k] == node, one, none)
            counts_t[start // unit + u] = seen

    def dense(start, self_rows, sum_rows):
        here = pl.ds(pl.multiple_of(start, part_rows), part_rows)
        self_first = self_rows[...].reshape(part_rows, width).astype(jnp.bfloat16)
        neigh_first = (sum_rows[...].reshape(part_rows, width) / fan_first).astype(jnp.bfloat16)
        first = jnp.concatenate([self_first, neigh_first], axis=1)
        first_all[here, :] = first
        pre = jnp.dot(first, w1_both[...], preferred_element_type=jnp.float32)
        square = pre * pre
        bend = jnp.tanh(GELU_SCALE * (pre + GELU_CUBE * (square * pre)))
        half_up = 0.5 * (1.0 + bend)
        hidden_all[here, :] = (pre * half_up).astype(jnp.bfloat16)
        slope_all[here, :] = half_up + (0.5 * GELU_SCALE) * pre * (1.0 - bend * bend) * (
            1.0 + (3.0 * GELU_CUBE) * square
        )

    @pl.loop(0, pairs)
    def _(pair):
        local = pair * (2 * part_rows)
        start = step * block + local
        gather(local, start, self_even, sum_even)
        dense(jnp.maximum(start - part_rows, part_rows), self_odd, sum_odd)
        gather(local + part_rows, start + part_rows, self_odd, sum_odd)
        dense(start, self_even, sum_even)

    @pl.when(step == steps - 1)
    def _():
        dense(middle - part_rows, self_odd, sum_odd)
        second_t[...] = jnp.zeros_like(second_t)

        @pl.loop(0, steps)
        def _(part):
            rows = pl.ds(pl.multiple_of(part * block, block), block)
            seen = counts_t[pl.ds(part * (block // unit), block // unit)].reshape(block, seeds)
            second_t[...] += dot_first(hidden_all[rows, :], seen)

        neigh_second = (jnp.transpose(second_t[...]) / fan_second).astype(jnp.bfloat16)
        seed_hidden = hidden_all[0:seeds, :]
        w2_self = w2_pad[0]
        w2_neigh = w2_pad[1]
        logits = dot_last(seed_hidden, w2_self) + dot_last(neigh_second, w2_neigh)
        column = lax.broadcasted_iota(jnp.int32, (seeds, padded), 1)
        real = column < classes
        log_total = jnp.log(
            jnp.sum(jnp.where(real, jnp.exp(logits), 0.0), axis=1, keepdims=True)
        )
        label = jnp.transpose(jnp.broadcast_to(labels_ref[...], (128, seeds)))
        label = jnp.concatenate([label] * (padded // 128), axis=1)
        onehot = jnp.where(column == label, 1.0, 0.0)
        picked = jnp.sum(onehot * logits, axis=1, keepdims=True)
        loss = jnp.broadcast_to(log_total - picked, (seeds, 128))
        loss_ref[...] = jnp.transpose(loss)[0:1, :]
        probs = jnp.where(real, jnp.exp(logits - log_total), 0.0)
        grad_logits = ((probs - onehot) / seeds).astype(jnp.bfloat16)
        term_self = dot_first(grad_logits, seed_hidden)
        term_neigh = dot_first(grad_logits, neigh_second)
        at = 4 * width
        high = -(-classes // 8) * 8
        grads_ref[at : at + high, :] = term_self[0:high, 0:128]
        grads_ref[at + high : at + 2 * high, :] = term_self[0:high, 128:256]
        grads_ref[at + 2 * high : at + 3 * high, :] = term_neigh[0:high, 0:128]
        grads_ref[at + 3 * high : at + 4 * high, :] = term_neigh[0:high, 128:256]
        rest = grads_ref.shape[0] - (at + 4 * high)
        if rest > 0:
            grads_ref[at + 4 * high :, :] = jnp.zeros((rest, 128), jnp.float32)
        back_second = (
            jnp.dot(grad_logits, w2_neigh, preferred_element_type=jnp.float32) / fan_second
        )
        back_high = back_second.astype(jnp.bfloat16)
        back_low = (back_second - back_high.astype(jnp.float32)).astype(jnp.bfloat16)
        seed_grad[...] = jnp.dot(grad_logits, w2_self, preferred_element_type=jnp.float32)
        grad_w1[...] = jnp.zeros_like(grad_w1)

        @pl.loop(0, middle // seeds)
        def _(part):
            rows = pl.ds(pl.multiple_of(part * seeds, seeds), seeds)
            seen = counts_t[pl.ds(part * (seeds // unit), seeds // unit)].reshape(seeds, seeds)
            grad = jnp.dot(seen, back_high, preferred_element_type=jnp.float32) + jnp.dot(
                seen, back_low, preferred_element_type=jnp.float32
            )
            own = jnp.where(part == 0, 1.0, 0.0)
            grad = grad + own * seed_grad[...]
            grad_pre = (grad * slope_all[rows, :]).astype(jnp.bfloat16)
            grad_w1[...] += dot_first(first_all[rows, :], grad_pre)

        grads_ref[0:width, :] = grad_w1[0:width, 0:128]
        grads_ref[width : 2 * width, :] = grad_w1[0:width, 128:256]
        grads_ref[2 * width : 3 * width, :] = grad_w1[width : 2 * width, 0:128]
        grads_ref[3 * width : 4 * width, :] = grad_w1[width : 2 * width, 128:256]


def sage_step(hot_rows, cold_rows, counts, mid_self, nbr1, nbr2, labels, weights):
    w1_self, w1_neigh, w2_self, w2_neigh = weights
    seeds = labels.shape[1]
    middle = mid_self.shape[1]
    fan_first, fan_second = nbr1.shape[1], nbr2.shape[1]
    width, hidden = w1_self.shape
    block = 3 * seeds
    steps = middle // block
    unit, units = 16, 4
    table_rows = hot_rows.shape[0] + cold_rows.shape[0] * cold_rows.shape[1]
    positions = nbr1.reshape(fan_first, steps, block).transpose(1, 0, 2).reshape(-1)
    vmem = pl.BlockSpec(memory_space=pltpu.VMEM)
    smem = pl.BlockSpec(memory_space=pltpu.SMEM)
    rows_buffer = pltpu.VMEM((units, unit, width), jnp.float32)
    return pl.pallas_call(
        sage_kernel,
        grid=(steps,),
        out_shape=(
            jax.ShapeDtypeStruct((1, seeds), jnp.float32),
            jax.ShapeDtypeStruct((GRAD_ROWS, 128), jnp.float32),
        ),
        in_specs=[
            smem,
            smem,
            pl.BlockSpec((fan_first * block,), lambda i: (i,), memory_space=pltpu.SMEM),
        ]
        + [vmem] * 8,
        out_specs=(vmem, vmem),
        scratch_shapes=[
            pltpu.VMEM((table_rows, 1, width), jnp.float32),
            pltpu.VMEM((fan_second, unit, seeds), jnp.int16),
            rows_buffer,
            rows_buffer,
            rows_buffer,
            rows_buffer,
            pltpu.VMEM((middle, 2 * width), jnp.bfloat16),
            pltpu.VMEM((middle, hidden), jnp.float32),
            pltpu.VMEM((middle, hidden), jnp.bfloat16),
            pltpu.VMEM((middle // unit, unit, seeds), jnp.bfloat16),
            pltpu.VMEM((hidden, seeds), jnp.float32),
            pltpu.VMEM((seeds, hidden), jnp.float32),
            pltpu.VMEM((2 * width, hidden), jnp.bfloat16),
            pltpu.VMEM((2, 256, hidden), jnp.bfloat16),
            pltpu.VMEM((2 * width, hidden), jnp.float32),
        ],
        compiler_params=pltpu.CompilerParams(vmem_limit_bytes=52 * 1024 * 1024),
        name="sage_step",
    )(
        counts, mid_self.reshape(-1), positions,
        hot_rows, cold_rows, nbr2, labels, w1_self, w1_neigh, w2_self.T, w2_neigh.T,
    )


def fetch_kernel(
    cliques,
    groups,
    hot_table,
    cold_table,
    hot_ids_ref,
    cold_ids_ref,
    hot_out,
    cold_out,
    hot_raw,
    cold_raw,
    hot_wide,
    cold_wide,
    hot_ask,
    cold_ask,
    hot_req,
    cold_req,
    hot_req_s,
    cold_req_s,
    hot_stage,
    cold_stage,
    hot_send,
    cold_send,
    local_sems,
    hot_id_sems,
    cold_id_sems,
    hot_row_sems,
    cold_row_sems,
):
    c = lax.axis_index("clique")
    g = lax.axis_index("group")

    def clique_at(d):
        return (lax.rem(c + d, cliques), g)

    def group_at(d):
        return (c, lax.rem(g + d, groups))

    load_cold = pltpu.make_async_copy(cold_table, cold_raw, local_sems.at[0])
    load_hot = pltpu.make_async_copy(hot_table, hot_raw, local_sems.at[1])
    load_cold.start()
    load_hot.start()

    barrier = pltpu.get_barrier_semaphore()

    @pl.loop(1, cliques)
    def _(d):
        pl.semaphore_signal(barrier, inc=1, device_id=clique_at(d), device_id_type=MESH)

    @pl.loop(1, groups)
    def _(d):
        pl.semaphore_signal(barrier, inc=1, device_id=group_at(d), device_id_type=MESH)

    for j in range(cliques):
        hot_ask[j] = hot_ids_ref[0, j : j + 1, :]
    for o in range(groups):
        cold_ask[o] = cold_ids_ref[0, o : o + 1, :]
    hot_req[c] = hot_ask[c]
    cold_req[g] = cold_ask[g]
    pl.semaphore_wait(barrier, cliques + groups - 2)

    def remote(source, target, sems, d, device):
        return pltpu.make_async_remote_copy(
            src_ref=source,
            dst_ref=target,
            send_sem=sems.at[0, d - 1],
            recv_sem=sems.at[1, d - 1],
            device_id=device,
            device_id_type=MESH,
        )

    def ask_cold(d):
        peer = lax.rem(g + d, groups)
        return remote(cold_ask.at[peer], cold_req.at[g], cold_id_sems, d, group_at(d))

    def ask_hot(d):
        peer = lax.rem(c + d, cliques)
        return remote(hot_ask.at[peer], hot_req.at[c], hot_id_sems, d, clique_at(d))

    def give_cold(d):
        peer = lax.rem(g + groups - d, groups)
        return remote(
            cold_send.at[peer], cold_out.at[g], cold_row_sems, d, group_at(groups - d)
        )

    def give_hot(d):
        peer = lax.rem(c + cliques - d, cliques)
        return remote(
            hot_send.at[peer], hot_out.at[c], hot_row_sems, d, clique_at(cliques - d)
        )

    @pl.loop(1, groups)
    def _(d):
        ask_cold(d).start()

    @pl.loop(1, cliques)
    def _(d):
        ask_hot(d).start()

    def widen(raw, wide):
        rows = 256

        @pl.loop(0, raw.shape[0] // rows)
        def _(part):
            here = pl.ds(pl.multiple_of(part * rows, rows), rows)
            wide[here, :] = raw[here, :].astype(jnp.float32)

    def gather(wide, wanted, who, stage):
        units, unit, width = stage.shape

        @pl.loop(0, units)
        def _(part):
            for r in range(unit):
                stage[part, r : r + 1, :] = wide[pl.ds(wanted[who, 0, part * unit + r], 1), :]

        return stage[...].reshape(units * unit, width).astype(jnp.bfloat16)

    load_cold.wait()
    widen(cold_raw, cold_wide)

    @pl.loop(1, groups)
    def _(d):
        ask_cold(d).wait()

    to_scalars = pltpu.make_async_copy(cold_req, cold_req_s, local_sems.at[2])
    to_scalars.start()
    to_scalars.wait()

    @pl.loop(1, groups)
    def _(d):
        peer = lax.rem(g + groups - d, groups)
        cold_send[peer] = gather(cold_wide, cold_req_s, peer, cold_stage)
        give_cold(d).start()

    load_hot.wait()
    widen(hot_raw, hot_wide)

    @pl.loop(1, cliques)
    def _(d):
        ask_hot(d).wait()

    to_scalars = pltpu.make_async_copy(hot_req, hot_req_s, local_sems.at[3])
    to_scalars.start()
    to_scalars.wait()

    @pl.loop(1, cliques)
    def _(d):
        peer = lax.rem(c + cliques - d, cliques)
        hot_send[peer] = gather(hot_wide, hot_req_s, peer, hot_stage)
        give_hot(d).start()

    hot_out[c] = gather(hot_wide, hot_req_s, c, hot_stage)
    cold_out[g] = gather(cold_wide, cold_req_s, g, cold_stage)

    @pl.loop(1, cliques)
    def _(d):
        give_hot(d).wait()

    @pl.loop(1, groups)
    def _(d):
        give_cold(d).wait()


def fetch_rows(hot_shard, cold_shard, hot_ids, cold_ids, cliques, groups):
    width = hot_shard.shape[1]
    hot_slots, cold_slots = hot_ids.shape[2], cold_ids.shape[2]
    vmem = pl.BlockSpec(memory_space=pltpu.VMEM)
    anywhere = pl.BlockSpec(memory_space=pl.ANY)
    bf16, f32, i32 = jnp.bfloat16, jnp.float32, jnp.int32
    return pl.pallas_call(
        partial(fetch_kernel, cliques, groups),
        out_shape=(
            jax.ShapeDtypeStruct((cliques, hot_slots, width), bf16),
            jax.ShapeDtypeStruct((groups, cold_slots, width), bf16),
        ),
        in_specs=[anywhere, anywhere, vmem, vmem],
        out_specs=(vmem, vmem),
        scratch_shapes=[
            pltpu.VMEM(hot_shard.shape, bf16),
            pltpu.VMEM(cold_shard.shape, bf16),
            pltpu.VMEM(hot_shard.shape, f32),
            pltpu.VMEM(cold_shard.shape, f32),
            pltpu.VMEM((cliques, 1, hot_slots), i32),
            pltpu.VMEM((groups, 1, cold_slots), i32),
            pltpu.VMEM((cliques, 1, hot_slots), i32),
            pltpu.VMEM((groups, 1, cold_slots), i32),
            pltpu.SMEM((cliques, 1, hot_slots), i32),
            pltpu.SMEM((groups, 1, cold_slots), i32),
            pltpu.VMEM((hot_slots // 16, 16, width), f32),
            pltpu.VMEM((cold_slots // 16, 16, width), f32),
            pltpu.VMEM((cliques, hot_slots, width), bf16),
            pltpu.VMEM((groups, cold_slots, width), bf16),
            pltpu.SemaphoreType.DMA((4,)),
            pltpu.SemaphoreType.DMA((2, cliques - 1)),
            pltpu.SemaphoreType.DMA((2, groups - 1)),
            pltpu.SemaphoreType.DMA((2, cliques - 1)),
            pltpu.SemaphoreType.DMA((2, groups - 1)),
        ],
        compiler_params=pltpu.CompilerParams(
            collective_id=1, has_side_effects=True, vmem_limit_bytes=48 * 1024 * 1024
        ),
        name="fetch_rows",
    )(hot_shard, cold_shard, hot_ids, cold_ids)


def reduce_kernel(
    cliques,
    groups,
    term_ref,
    w1_self_ref,
    w1_neigh_ref,
    w2_self_ref,
    w2_neigh_ref,
    whole,
    pair_in,
    clique_in,
    chip_in,
    half_sum,
    back,
    pair_sems,
    clique_sems,
    chip_sems,
):
    chips = groups // 2
    c = lax.axis_index("clique")
    g = lax.axis_index("group")
    core = lax.rem(g, 2)
    chip = g // 2
    rows = whole.shape[0]
    per_pair = rows // 2
    per_clique = per_pair // cliques
    per_chip = per_clique // chips

    def pair():
        return (c, chip * 2 + 1 - core)

    def clique(d):
        return (lax.rem(c + d, cliques), g)

    def other_chip(d):
        return (c, lax.rem(chip + d, chips) * 2 + core)

    def rows_at(start, size):
        return pl.ds(pl.multiple_of(start, 8), size)

    def send(source, target, sems, number, device):
        copy = pltpu.make_async_remote_copy(
            src_ref=source,
            dst_ref=target,
            send_sem=sems.at[0, number],
            recv_sem=sems.at[1, number],
            device_id=device,
            device_id_type=MESH,
        )
        copy.start()
        return copy

    barrier = pltpu.get_barrier_semaphore()
    partners = [pair()]
    partners += [clique(d) for d in range(1, cliques)]
    partners += [other_chip(d) for d in range(1, chips)]
    for device in partners:
        pl.semaphore_signal(barrier, inc=1, device_id=device, device_id_type=MESH)
    terms = term_ref.shape[0]
    whole[0:terms, :] = term_ref[...]
    if rows > terms:
        whole[terms:rows, :] = jnp.zeros((rows - terms, 128), jnp.float32)
    pl.semaphore_wait(barrier, len(partners))

    pair_start = core * per_pair
    mine = pair_start + c * per_clique
    own = mine + chip * per_chip

    copy = send(
        whole.at[rows_at((1 - core) * per_pair, per_pair)], pair_in, pair_sems, 0, pair()
    )
    copy.wait()
    half = rows_at(pair_start, per_pair)
    half_sum[half, :] = whole[half, :] + pair_in[...]

    copies = []
    for d in range(1, cliques):
        peer = lax.rem(c + d, cliques)
        part = rows_at(pair_start + peer * per_clique, per_clique)
        copies.append(send(half_sum.at[part], clique_in.at[d - 1], clique_sems, d - 1, clique(d)))
    for copy in copies:
        copy.wait()
    part = rows_at(mine, per_clique)
    total = half_sum[part, :]
    for d in range(1, cliques):
        total = total + clique_in[d - 1]
    whole[part, :] = total

    copies = []
    for d in range(1, chips):
        peer = lax.rem(chip + d, chips)
        part = rows_at(mine + peer * per_chip, per_chip)
        copies.append(send(whole.at[part], chip_in.at[d - 1], chip_sems, d - 1, other_chip(d)))
    for copy in copies:
        copy.wait()
    part = rows_at(own, per_chip)
    total = whole[part, :]
    for d in range(1, chips):
        total = total + chip_in[d - 1]
    back[part, :] = total

    copies = []
    for d in range(1, chips):
        copies.append(
            send(back.at[part], back.at[part], chip_sems, chips - 2 + d, other_chip(d))
        )
    for copy in copies:
        copy.wait()
    part = rows_at(mine, per_clique)
    copies = []
    for d in range(1, cliques):
        copies.append(
            send(back.at[part], back.at[part], clique_sems, cliques - 2 + d, clique(d))
        )
    for copy in copies:
        copy.wait()
    part = rows_at(pair_start, per_pair)
    copy = send(back.at[part], back.at[part], pair_sems, 1, pair())
    copy.wait()

    width, hidden = w1_self_ref.shape
    classes = w2_self_ref.shape[0]
    high = -(-classes // 8) * 8
    w1_self_ref[:, 0:128] = back[0:width, :]
    w1_self_ref[:, 128:256] = back[width : 2 * width, :]
    w1_neigh_ref[:, 0:128] = back[2 * width : 3 * width, :]
    w1_neigh_ref[:, 128:256] = back[3 * width : 4 * width, :]
    at = 4 * width
    w2_self_ref[:, 0:128] = back[at : at + classes, :]
    w2_self_ref[:, 128:256] = back[at + high : at + high + classes, :]
    w2_neigh_ref[:, 0:128] = back[at + 2 * high : at + 2 * high + classes, :]
    w2_neigh_ref[:, 128:256] = back[at + 3 * high : at + 3 * high + classes, :]


def reduce_terms(terms, shapes, cliques, groups):
    chips = groups // 2
    unit = 8 * 2 * cliques * chips
    rows = -(-terms.shape[0] // unit) * unit
    per_clique = rows // 2 // cliques
    vmem = pl.BlockSpec(memory_space=pltpu.VMEM)
    return pl.pallas_call(
        partial(reduce_kernel, cliques, groups),
        out_shape=tuple(jax.ShapeDtypeStruct(shape, jnp.float32) for shape in shapes),
        in_specs=[vmem],
        out_specs=(vmem,) * len(shapes),
        scratch_shapes=[
            pltpu.VMEM((rows, 128), jnp.float32),
            pltpu.VMEM((rows // 2, 128), jnp.float32),
            pltpu.VMEM((cliques - 1, per_clique, 128), jnp.float32),
            pltpu.VMEM((chips - 1, per_clique // chips, 128), jnp.float32),
            pltpu.VMEM((rows, 128), jnp.float32),
            pltpu.VMEM((rows, 128), jnp.float32),
            pltpu.SemaphoreType.DMA((2, 2)),
            pltpu.SemaphoreType.DMA((2, 2 * (cliques - 1))),
            pltpu.SemaphoreType.DMA((2, 2 * (chips - 1))),
        ],
        compiler_params=pltpu.CompilerParams(
            collective_id=0, has_side_effects=True, vmem_limit_bytes=32 * 1024 * 1024
        ),
        name="reduce_terms",
    )(terms)


def body(
    cliques,
    groups,
    hot_shard,
    cold_shard,
    hot_ids,
    cold_ids,
    cold_counts,
    mid_self,
    nbr1,
    nbr2,
    labels,
    w1_self,
    w1_neigh,
    w2_self,
    w2_neigh,
):
    hot_rows, cold_rows = fetch_rows(hot_shard, cold_shard, hot_ids, cold_ids, cliques, groups)
    seed_loss, terms = sage_step(
        hot_rows.reshape(-1, hot_shard.shape[1]), cold_rows, cold_counts, mid_self, nbr1, nbr2, labels,
        (w1_self, w1_neigh, w2_self, w2_neigh),
    )
    shapes = (w1_self.shape, w1_neigh.shape, w2_self.T.shape, w2_neigh.T.shape)
    totals = reduce_terms(terms, shapes, cliques, groups)
    return (seed_loss, totals[0], totals[1], totals[2].T, totals[3].T)


def solution(mesh):
    return jax.shard_map(
        partial(body, mesh.shape["clique"], mesh.shape["group"]),
        mesh=mesh,
        in_specs=(
            P("clique", None),
            P("group", None),
            P(("clique", "group"), None, None),
            P(("clique", "group"), None, None),
            P(("clique", "group"), None),
            P(("clique", "group"), None),
            P(("clique", "group"), None, None),
            P(("clique", "group"), None, None),
            P(("clique", "group"), None),
            P(),
            P(),
            P(),
            P(),
        ),
        out_specs=(P(("clique", "group"), None), P(), P(), P(), P()),
        check_vma=False,
    )
```

```python
from functools import partial

import jax
import jax.numpy as jnp
from jax import lax
from jax.experimental import pallas as pl
from jax.experimental.pallas import tpu as pltpu
from jax.sharding import PartitionSpec as P

GELU_SCALE = 0.7978845608028654
GELU_CUBE = 0.044715
GRAD_ROWS = 1280
MESH = pl.DeviceIdType.MESH


def dot_first(left, right):
    return lax.dot_general(
        left, right, (((0,), (0,)), ((), ())), preferred_element_type=jnp.float32
    )


def dot_last(left, right):
    return lax.dot_general(
        left, right, (((1,), (1,)), ((), ())), preferred_element_type=jnp.float32
    )


def sage_kernel(
    counts_ref,
    self_ref,
    nbr1_ref,
    hot_ref,
    cold_ref,
    nbr2_ref,
    labels_ref,
    w1_self_ref,
    w1_neigh_ref,
    w2_self_ref,
    w2_neigh_ref,
    loss_ref,
    grads_ref,
    table,
    spread_ids,
    self_even,
    sum_even,
    self_odd,
    sum_odd,
    first_all,
    slope_all,
    hidden_all,
    counts_t,
    second_t,
    seed_grad,
    w1_both,
    w2_pad,
    grad_w1,
):
    step = pl.program_id(0)
    steps = pl.num_programs(0)
    units, unit, width = sum_even.shape
    part_rows = units * unit
    middle = first_all.shape[0]
    block = middle // steps
    pairs = block // (2 * part_rows)
    fan_first = nbr1_ref.shape[0]
    fan_second, seeds = nbr2_ref.shape[0], nbr2_ref.shape[2]
    owners, slots, _ = cold_ref.shape
    hot_rows = hot_ref.shape[0]
    hidden = w1_self_ref.shape[1]
    classes = w2_self_ref.shape[0]
    padded = w2_pad.shape[1]
    count_type = spread_ids.dtype

    @pl.when(step == 0)
    def _():
        @pl.loop(0, hot_rows // 16)
        def _(part):
            rows = hot_ref[pl.ds(pl.multiple_of(part * 16, 16), 16), :].astype(jnp.float32)
            for r in range(16):
                table[part * 16 + r] = rows[r : r + 1, :]

        @pl.loop(0, owners)
        def _(owner):
            live = lax.broadcasted_iota(jnp.int32, (slots, width), 0) < counts_ref[0, owner]
            rows = jnp.where(live, cold_ref[owner].astype(jnp.float32), 0.0)
            for r in range(slots):
                table[hot_rows + owner * slots + r] = rows[r : r + 1, :]

        for k in range(fan_second):
            spread_ids[k] = jnp.broadcast_to(nbr2_ref[k], (unit, seeds)).astype(
                count_type
            )
        w1_both[0:width, :] = w1_self_ref[...]
        w1_both[width : 2 * width, :] = w1_neigh_ref[...]
        w2_pad[...] = jnp.zeros_like(w2_pad)
        w2_pad[0, 0:classes, :] = w2_self_ref[...]
        w2_pad[1, 0:classes, :] = w2_neigh_ref[...]
        self_odd[...] = jnp.zeros_like(self_odd)
        sum_odd[...] = jnp.zeros_like(sum_odd)

    def gather(near, own, offset, start, self_rows, sum_rows):
        for u in range(units):
            for r in range(unit):
                at = offset + u * unit + r
                total = table[near[0][at]]
                for k in range(1, fan_first):
                    total = total + table[near[k][at]]
                sum_rows[u, r : r + 1, :] = total
                self_rows[u, r : r + 1, :] = table[own[at]]
            node = (
                lax.broadcasted_iota(jnp.int32, (unit, seeds), 0) + (start + u * unit)
            ).astype(count_type)
            seen = jnp.zeros((unit, seeds), jnp.bfloat16)
            one = jnp.ones((unit, seeds), jnp.bfloat16)
            none = jnp.zeros((unit, seeds), jnp.bfloat16)
            for k in range(fan_second):
                seen = seen + jnp.where(spread_ids[k] == node, one, none)
            counts_t[start // unit + u] = seen

    def dense(start, self_rows, sum_rows):
        here = pl.ds(pl.multiple_of(start, part_rows), part_rows)
        self_first = self_rows[...].reshape(part_rows, width).astype(jnp.bfloat16)
        neigh_first = (sum_rows[...].reshape(part_rows, width) / fan_first).astype(jnp.bfloat16)
        first = jnp.concatenate([self_first, neigh_first], axis=1)
        first_all[here, :] = first
        pre = jnp.dot(first, w1_both[...], preferred_element_type=jnp.float32)
        square = pre * pre
        bend = jnp.tanh(GELU_SCALE * (pre + GELU_CUBE * (square * pre)))
        half_up = 0.5 * (1.0 + bend)
        hidden_all[here, :] = (pre * half_up).astype(jnp.bfloat16)
        slope_all[here, :] = half_up + (0.5 * GELU_SCALE) * pre * (1.0 - bend * bend) * (
            1.0 + (3.0 * GELU_CUBE) * square
        )

    @pl.loop(0, pairs)
    def _(pair):
        span = 2 * part_rows
        local = pl.multiple_of(pair * span, span)
        start = pl.multiple_of(step * block + local, span)
        near = [nbr1_ref.at[k, 0, pl.ds(local, span)] for k in range(fan_first)]
        own = self_ref.at[0, pl.ds(start, span)]
        gather(near, own, 0, start, self_even, sum_even)
        dense(jnp.maximum(start - part_rows, part_rows), self_odd, sum_odd)
        gather(near, own, part_rows, start + part_rows, self_odd, sum_odd)
        dense(start, self_even, sum_even)

    @pl.when(step == steps - 1)
    def _():
        dense(middle - part_rows, self_odd, sum_odd)
        second_t[...] = jnp.zeros_like(second_t)

        @pl.loop(0, steps)
        def _(part):
            rows = pl.ds(pl.multiple_of(part * block, block), block)
            seen = counts_t[pl.ds(part * (block // unit), block // unit)].reshape(block, seeds)
            second_t[...] += dot_first(hidden_all[rows, :], seen)

        neigh_second = (jnp.transpose(second_t[...]) / fan_second).astype(jnp.bfloat16)
        seed_hidden = hidden_all[0:seeds, :]
        w2_self = w2_pad[0]
        w2_neigh = w2_pad[1]
        logits = dot_last(seed_hidden, w2_self) + dot_last(neigh_second, w2_neigh)
        column = lax.broadcasted_iota(jnp.int32, (seeds, padded), 1)
        real = column < classes
        log_total = jnp.log(
            jnp.sum(jnp.where(real, jnp.exp(logits), 0.0), axis=1, keepdims=True)
        )
        label = jnp.transpose(jnp.broadcast_to(labels_ref[...], (128, seeds)))
        label = jnp.concatenate([label] * (padded // 128), axis=1)
        onehot = jnp.where(column == label, 1.0, 0.0)
        picked = jnp.sum(onehot * logits, axis=1, keepdims=True)
        loss = jnp.broadcast_to(log_total - picked, (seeds, 128))
        loss_ref[...] = jnp.transpose(loss)[0:1, :]
        probs = jnp.where(real, jnp.exp(logits - log_total), 0.0)
        grad_logits = ((probs - onehot) / seeds).astype(jnp.bfloat16)
        term_self = dot_first(grad_logits, seed_hidden)
        term_neigh = dot_first(grad_logits, neigh_second)
        at = 4 * width
        high = -(-classes // 8) * 8
        grads_ref[at : at + high, :] = term_self[0:high, 0:128]
        grads_ref[at + high : at + 2 * high, :] = term_self[0:high, 128:256]
        grads_ref[at + 2 * high : at + 3 * high, :] = term_neigh[0:high, 0:128]
        grads_ref[at + 3 * high : at + 4 * high, :] = term_neigh[0:high, 128:256]
        rest = grads_ref.shape[0] - (at + 4 * high)
        if rest > 0:
            grads_ref[at + 4 * high :, :] = jnp.zeros((rest, 128), jnp.float32)
        back_second = (
            jnp.dot(grad_logits, w2_neigh, preferred_element_type=jnp.float32) / fan_second
        )
        back_high = back_second.astype(jnp.bfloat16)
        back_low = (back_second - back_high.astype(jnp.float32)).astype(jnp.bfloat16)
        seed_grad[...] = jnp.dot(grad_logits, w2_self, preferred_element_type=jnp.float32)
        grad_w1[...] = jnp.zeros_like(grad_w1)

        @pl.loop(0, middle // seeds, unroll=3)
        def _(part):
            rows = pl.ds(pl.multiple_of(part * seeds, seeds), seeds)
            seen = counts_t[pl.ds(part * (seeds // unit), seeds // unit)].reshape(seeds, seeds)
            grad = jnp.dot(seen, back_high, preferred_element_type=jnp.float32) + jnp.dot(
                seen, back_low, preferred_element_type=jnp.float32
            )
            own = jnp.where(part == 0, 1.0, 0.0)
            grad = grad + own * seed_grad[...]
            grad_pre = (grad * slope_all[rows, :]).astype(jnp.bfloat16)
            grad_w1[...] += dot_first(first_all[rows, :], grad_pre)

        grads_ref[0:width, :] = grad_w1[0:width, 0:128]
        grads_ref[width : 2 * width, :] = grad_w1[0:width, 128:256]
        grads_ref[2 * width : 3 * width, :] = grad_w1[width : 2 * width, 0:128]
        grads_ref[3 * width : 4 * width, :] = grad_w1[width : 2 * width, 128:256]


def sage_step(hot_rows, cold_rows, counts, mid_self, nbr1, nbr2, labels, weights):
    w1_self, w1_neigh, w2_self, w2_neigh = weights
    seeds = labels.shape[1]
    middle = mid_self.shape[1]
    fan_first, fan_second = nbr1.shape[1], nbr2.shape[1]
    width, hidden = w1_self.shape
    block = 3 * seeds
    steps = middle // block
    unit, units = 16, 4
    table_rows = hot_rows.shape[0] + cold_rows.shape[0] * cold_rows.shape[1]
    vmem = pl.BlockSpec(memory_space=pltpu.VMEM)
    smem = pl.BlockSpec(memory_space=pltpu.SMEM)
    rows_buffer = pltpu.VMEM((units, unit, width), jnp.float32)
    return pl.pallas_call(
        sage_kernel,
        grid=(steps,),
        out_shape=(
            jax.ShapeDtypeStruct((1, seeds), jnp.float32),
            jax.ShapeDtypeStruct((GRAD_ROWS, 128), jnp.float32),
        ),
        in_specs=[
            smem,
            smem,
            pl.BlockSpec((fan_first, 1, block), lambda i: (0, 0, i), memory_space=pltpu.SMEM),
        ]
        + [vmem] * 8,
        out_specs=(vmem, vmem),
        scratch_shapes=[
            pltpu.VMEM((table_rows, 1, width), jnp.float32),
            pltpu.VMEM((fan_second, unit, seeds), jnp.int16),
            rows_buffer,
            rows_buffer,
            rows_buffer,
            rows_buffer,
            pltpu.VMEM((middle, 2 * width), jnp.bfloat16),
            pltpu.VMEM((middle, hidden), jnp.float32),
            pltpu.VMEM((middle, hidden), jnp.bfloat16),
            pltpu.VMEM((middle // unit, unit, seeds), jnp.bfloat16),
            pltpu.VMEM((hidden, seeds), jnp.float32),
            pltpu.VMEM((seeds, hidden), jnp.float32),
            pltpu.VMEM((2 * width, hidden), jnp.bfloat16),
            pltpu.VMEM((2, 256, hidden), jnp.bfloat16),
            pltpu.VMEM((2 * width, hidden), jnp.float32),
        ],
        compiler_params=pltpu.CompilerParams(vmem_limit_bytes=40 * 1024 * 1024),
        name="sage_step",
    )(
        counts, mid_self, nbr1.transpose(1, 0, 2),
        hot_rows, cold_rows, nbr2.transpose(1, 0, 2), labels, w1_self, w1_neigh, w2_self.T, w2_neigh.T,
    )


def fetch_kernel(
    cliques,
    groups,
    hot_table,
    cold_table,
    hot_ids,
    cold_ids,
    hot_out,
    cold_out,
    hot_ids_ref,
    cold_ids_ref,
    hot_raw,
    cold_raw,
    hot_wide,
    cold_wide,
    hot_ask,
    cold_ask,
    hot_req,
    cold_req,
    hot_req_s,
    cold_req_s,
    hot_stage,
    cold_stage,
    hot_send,
    cold_send,
    local_sems,
    hot_id_sems,
    cold_id_sems,
    hot_row_sems,
    cold_row_sems,
):
    c = lax.axis_index("clique")
    g = lax.axis_index("group")

    def clique_at(d):
        return (lax.rem(c + d, cliques), g)

    def group_at(d):
        return (c, lax.rem(g + d, groups))

    load_ids = [
        pltpu.make_async_copy(hot_ids, hot_ids_ref, local_sems.at[4]),
        pltpu.make_async_copy(cold_ids, cold_ids_ref, local_sems.at[5]),
    ]
    for load in load_ids:
        load.start()
    load_cold = pltpu.make_async_copy(cold_table, cold_raw, local_sems.at[0])
    load_hot = pltpu.make_async_copy(hot_table, hot_raw, local_sems.at[1])
    load_cold.start()
    load_hot.start()

    barrier = pltpu.get_barrier_semaphore()

    @pl.loop(1, cliques)
    def _(d):
        pl.semaphore_signal(barrier, inc=1, device_id=clique_at(d), device_id_type=MESH)

    @pl.loop(1, groups)
    def _(d):
        pl.semaphore_signal(barrier, inc=1, device_id=group_at(d), device_id_type=MESH)

    for load in load_ids:
        load.wait()
    for j in range(cliques):
        hot_ask[j] = hot_ids_ref[0, j : j + 1, :]
    for o in range(groups):
        cold_ask[o] = cold_ids_ref[0, o : o + 1, :]
    hot_req[c] = hot_ask[c]
    cold_req[g] = cold_ask[g]
    pl.semaphore_wait(barrier, cliques + groups - 2)

    def remote(source, target, sems, d, device):
        return pltpu.make_async_remote_copy(
            src_ref=source,
            dst_ref=target,
            send_sem=sems.at[0, d - 1],
            recv_sem=sems.at[1, d - 1],
            device_id=device,
            device_id_type=MESH,
        )

    def ask_cold(d):
        peer = lax.rem(g + d, groups)
        return remote(cold_ask.at[peer], cold_req.at[g], cold_id_sems, d, group_at(d))

    def ask_hot(d):
        peer = lax.rem(c + d, cliques)
        return remote(hot_ask.at[peer], hot_req.at[c], hot_id_sems, d, clique_at(d))

    def give_cold(d):
        peer = lax.rem(g + groups - d, groups)
        return remote(
            cold_send.at[peer], cold_out.at[g], cold_row_sems, d, group_at(groups - d)
        )

    def give_hot(d):
        peer = lax.rem(c + cliques - d, cliques)
        return remote(
            hot_send.at[peer], hot_out.at[c], hot_row_sems, d, clique_at(cliques - d)
        )

    @pl.loop(1, groups)
    def _(d):
        ask_cold(d).start()

    @pl.loop(1, cliques)
    def _(d):
        ask_hot(d).start()

    def widen(raw, wide):
        rows = 256

        @pl.loop(0, raw.shape[0] // rows)
        def _(part):
            here = pl.ds(pl.multiple_of(part * rows, rows), rows)
            wide[here, :] = raw[here, :].astype(jnp.float32)

    def gather(wide, wanted, who, stage):
        units, unit, width = stage.shape
        slots = units * unit
        span = min(slots, 128)

        @pl.loop(0, slots // span)
        def _(part):
            near = wanted.at[who, 0, pl.ds(pl.multiple_of(part * span, span), span)]
            for r in range(span):
                at = part * (span // unit) + r // unit
                stage[at, r % unit : r % unit + 1, :] = wide[pl.ds(near[r], 1), :]

        return stage[...].reshape(units * unit, width).astype(jnp.bfloat16)

    load_cold.wait()
    widen(cold_raw, cold_wide)

    @pl.loop(1, groups)
    def _(d):
        ask_cold(d).wait()

    to_scalars = pltpu.make_async_copy(cold_req, cold_req_s, local_sems.at[2])
    to_scalars.start()
    to_scalars.wait()

    @pl.loop(0, groups - 1)
    def _(e):
        d = lax.rem(e + groups // 2 - 1, groups - 1) + 1
        peer = lax.rem(g + groups - d, groups)
        cold_send[peer] = gather(cold_wide, cold_req_s, peer, cold_stage)
        give_cold(d).start()

    load_hot.wait()
    widen(hot_raw, hot_wide)

    @pl.loop(1, cliques)
    def _(d):
        ask_hot(d).wait()

    to_scalars = pltpu.make_async_copy(hot_req, hot_req_s, local_sems.at[3])
    to_scalars.start()
    to_scalars.wait()

    @pl.loop(1, cliques)
    def _(d):
        peer = lax.rem(c + cliques - d, cliques)
        hot_send[peer] = gather(hot_wide, hot_req_s, peer, hot_stage)
        give_hot(d).start()

    hot_out[c] = gather(hot_wide, hot_req_s, c, hot_stage)
    cold_out[g] = gather(cold_wide, cold_req_s, g, cold_stage)

    @pl.loop(1, cliques)
    def _(d):
        give_hot(d).wait()

    @pl.loop(1, groups)
    def _(d):
        give_cold(d).wait()


def fetch_rows(hot_shard, cold_shard, hot_ids, cold_ids, cliques, groups):
    width = hot_shard.shape[1]
    hot_slots, cold_slots = hot_ids.shape[2], cold_ids.shape[2]
    vmem = pl.BlockSpec(memory_space=pltpu.VMEM)
    hbm = pl.BlockSpec(memory_space=pltpu.HBM)
    bf16, f32, i32 = jnp.bfloat16, jnp.float32, jnp.int32
    return pl.pallas_call(
        partial(fetch_kernel, cliques, groups),
        out_shape=(
            jax.ShapeDtypeStruct((cliques, hot_slots, width), bf16),
            jax.ShapeDtypeStruct((groups, cold_slots, width), bf16),
        ),
        in_specs=[hbm, hbm, hbm, hbm],
        out_specs=(vmem, vmem),
        scratch_shapes=[
            pltpu.VMEM(hot_ids.shape, i32),
            pltpu.VMEM(cold_ids.shape, i32),
            pltpu.VMEM(hot_shard.shape, bf16),
            pltpu.VMEM(cold_shard.shape, bf16),
            pltpu.VMEM(hot_shard.shape, f32),
            pltpu.VMEM(cold_shard.shape, f32),
            pltpu.VMEM((cliques, 1, hot_slots), i32),
            pltpu.VMEM((groups, 1, cold_slots), i32),
            pltpu.VMEM((cliques, 1, hot_slots), i32),
            pltpu.VMEM((groups, 1, cold_slots), i32),
            pltpu.SMEM((cliques, 1, hot_slots), i32),
            pltpu.SMEM((groups, 1, cold_slots), i32),
            pltpu.VMEM((hot_slots // 16, 16, width), f32),
            pltpu.VMEM((cold_slots // 16, 16, width), f32),
            pltpu.VMEM((cliques, hot_slots, width), bf16),
            pltpu.VMEM((groups, cold_slots, width), bf16),
            pltpu.SemaphoreType.DMA((6,)),
            pltpu.SemaphoreType.DMA((2, cliques - 1)),
            pltpu.SemaphoreType.DMA((2, groups - 1)),
            pltpu.SemaphoreType.DMA((2, cliques - 1)),
            pltpu.SemaphoreType.DMA((2, groups - 1)),
        ],
        compiler_params=pltpu.CompilerParams(
            collective_id=1, has_side_effects=True, vmem_limit_bytes=102 * 512 * 1024
        ),
        name="fetch_rows",
    )(hot_shard, cold_shard, hot_ids, cold_ids)


def reduce_kernel(
    cliques,
    groups,
    term_ref,
    w1_self_ref,
    w1_neigh_ref,
    w2_self_ref,
    w2_neigh_ref,
    whole,
    pair_in,
    clique_in,
    chip_in,
    half_sum,
    back,
    pair_sems,
    clique_sems,
    chip_sems,
):
    chips = groups // 2
    c = lax.axis_index("clique")
    g = lax.axis_index("group")
    core = lax.rem(g, 2)
    chip = g // 2
    rows = whole.shape[0]
    per_pair = rows // 2
    per_clique = per_pair // cliques
    per_chip = per_clique // chips

    def pair():
        return (c, chip * 2 + 1 - core)

    def clique(d):
        return (lax.rem(c + d, cliques), g)

    def other_chip(d):
        return (c, lax.rem(chip + d, chips) * 2 + core)

    def rows_at(start, size):
        return pl.ds(pl.multiple_of(start, 8), size)

    def send(source, target, sems, number, device):
        copy = pltpu.make_async_remote_copy(
            src_ref=source,
            dst_ref=target,
            send_sem=sems.at[0, number],
            recv_sem=sems.at[1, number],
            device_id=device,
            device_id_type=MESH,
        )
        copy.start()
        return copy

    barrier = pltpu.get_barrier_semaphore()
    partners = [pair()]
    partners += [clique(d) for d in range(1, cliques)]
    partners += [other_chip(d) for d in range(1, chips)]
    for device in partners:
        pl.semaphore_signal(barrier, inc=1, device_id=device, device_id_type=MESH)
    terms = term_ref.shape[0]
    given = term_ref
    if rows > terms:
        whole[0:terms, :] = term_ref[...]
        whole[terms:rows, :] = jnp.zeros((rows - terms, 128), jnp.float32)
        given = whole
    pl.semaphore_wait(barrier, len(partners))

    pair_start = core * per_pair
    mine = pair_start + c * per_clique
    own = mine + chip * per_chip

    copy = send(
        given.at[rows_at((1 - core) * per_pair, per_pair)], pair_in, pair_sems, 0, pair()
    )
    copy.wait()
    half = rows_at(pair_start, per_pair)
    half_sum[half, :] = given[half, :] + pair_in[...]

    copies = []
    for d in range(1, cliques):
        peer = lax.rem(c + d, cliques)
        part = rows_at(pair_start + peer * per_clique, per_clique)
        copies.append(send(half_sum.at[part], clique_in.at[d - 1], clique_sems, d - 1, clique(d)))
    for copy in copies:
        copy.wait()
    part = rows_at(mine, per_clique)
    total = half_sum[part, :]
    for d in range(1, cliques):
        total = total + clique_in[d - 1]
    whole[part, :] = total

    copies = []
    for d in range(1, chips):
        peer = lax.rem(chip + d, chips)
        part = rows_at(mine + peer * per_chip, per_chip)
        copies.append(send(whole.at[part], chip_in.at[d - 1], chip_sems, d - 1, other_chip(d)))
    for copy in copies:
        copy.wait()
    part = rows_at(own, per_chip)
    total = whole[part, :]
    for d in range(1, chips):
        total = total + chip_in[d - 1]
    back[part, :] = total

    copies = []
    for d in range(1, chips):
        copies.append(
            send(back.at[part], back.at[part], chip_sems, chips - 2 + d, other_chip(d))
        )
    for copy in copies:
        copy.wait()
    part = rows_at(mine, per_clique)
    copies = []
    for d in range(1, cliques):
        copies.append(
            send(back.at[part], back.at[part], clique_sems, cliques - 2 + d, clique(d))
        )
    for copy in copies:
        copy.wait()
    part = rows_at(pair_start, per_pair)
    copy = send(back.at[part], back.at[part], pair_sems, 1, pair())
    copy.wait()

    width, hidden = w1_self_ref.shape
    classes = w2_self_ref.shape[0]
    high = -(-classes // 8) * 8
    w1_self_ref[:, 0:128] = back[0:width, :]
    w1_self_ref[:, 128:256] = back[width : 2 * width, :]
    w1_neigh_ref[:, 0:128] = back[2 * width : 3 * width, :]
    w1_neigh_ref[:, 128:256] = back[3 * width : 4 * width, :]
    at = 4 * width
    w2_self_ref[:, 0:128] = back[at : at + classes, :]
    w2_self_ref[:, 128:256] = back[at + high : at + high + classes, :]
    w2_neigh_ref[:, 0:128] = back[at + 2 * high : at + 2 * high + classes, :]
    w2_neigh_ref[:, 128:256] = back[at + 3 * high : at + 3 * high + classes, :]


def reduce_terms(terms, shapes, cliques, groups):
    chips = groups // 2
    unit = 8 * 2 * cliques * chips
    rows = -(-terms.shape[0] // unit) * unit
    per_clique = rows // 2 // cliques
    vmem = pl.BlockSpec(memory_space=pltpu.VMEM)
    return pl.pallas_call(
        partial(reduce_kernel, cliques, groups),
        out_shape=tuple(jax.ShapeDtypeStruct(shape, jnp.float32) for shape in shapes),
        in_specs=[vmem],
        out_specs=(vmem,) * len(shapes),
        scratch_shapes=[
            pltpu.VMEM((rows, 128), jnp.float32),
            pltpu.VMEM((rows // 2, 128), jnp.float32),
            pltpu.VMEM((cliques - 1, per_clique, 128), jnp.float32),
            pltpu.VMEM((chips - 1, per_clique // chips, 128), jnp.float32),
            pltpu.VMEM((rows, 128), jnp.float32),
            pltpu.VMEM((rows, 128), jnp.float32),
            pltpu.SemaphoreType.DMA((2, 2)),
            pltpu.SemaphoreType.DMA((2, 2 * (cliques - 1))),
            pltpu.SemaphoreType.DMA((2, 2 * (chips - 1))),
        ],
        compiler_params=pltpu.CompilerParams(
            collective_id=0, has_side_effects=True, vmem_limit_bytes=32 * 1024 * 1024
        ),
        name="reduce_terms",
    )(terms)


def body(
    cliques,
    groups,
    hot_shard,
    cold_shard,
    hot_ids,
    cold_ids,
    cold_counts,
    mid_self,
    nbr1,
    nbr2,
    labels,
    w1_self,
    w1_neigh,
    w2_self,
    w2_neigh,
):
    hot_rows, cold_rows = fetch_rows(hot_shard, cold_shard, hot_ids, cold_ids, cliques, groups)
    seed_loss, terms = sage_step(
        hot_rows.reshape(-1, hot_shard.shape[1]), cold_rows, cold_counts, mid_self, nbr1, nbr2, labels,
        (w1_self, w1_neigh, w2_self, w2_neigh),
    )
    shapes = (w1_self.shape, w1_neigh.shape, w2_self.T.shape, w2_neigh.T.shape)
    totals = reduce_terms(terms, shapes, cliques, groups)
    return (seed_loss, totals[0], totals[1], totals[2].T, totals[3].T)


def solution(mesh):
    return jax.shard_map(
        partial(body, mesh.shape["clique"], mesh.shape["group"]),
        mesh=mesh,
        in_specs=(
            P("clique", None),
            P("group", None),
            P(("clique", "group"), None, None),
            P(("clique", "group"), None, None),
            P(("clique", "group"), None),
            P(("clique", "group"), None),
            P(("clique", "group"), None, None),
            P(("clique", "group"), None, None),
            P(("clique", "group"), None),
            P(),
            P(),
            P(),
            P(),
        ),
        out_specs=(P(("clique", "group"), None), P(), P(), P(), P()),
        check_vma=False,
    )
```
